256 devices in a mesh: row: 8 (over y_hi, x), col: 32 (over z, y_lo, core).
Axes of the slice: x: 4, y: 4 (y_hi: 2, y_lo: 2; y = y_hi * 2 + y_lo), z: 8, core: 2. Of those that a mesh axis runs over, the one named last changes fastest.
Arguments:
- features: bfloat16 [65536, 128], P(('row', 'col')), may hold values from -6 to 6
- labels: int32 [65536], P(('row', 'col')), may hold values from 0 to 127
- train_mask: int32 [65536], P(('row', 'col')), may hold values from 0 to 1
- adj_rows: int32 [8, 32, 192], P('row', 'col'), may hold values from 0 to 15, as said below
- adj_cols: int32 [8, 32, 192], P('row', 'col'), may hold values from 0 to 63, as said below
- adj_live: int32 [8, 32], P('row', 'col'), may hold values from 1 to 192, as said below
- adj_values: bfloat16 [8, 32, 192, 128, 128], P('row', 'col'), may hold values from -0.0390625 to 0.0390625
- w_first: bfloat16 [128, 256], replicated, may hold values from -0.5 to 0.5
- b_first: float32 [256], replicated, may hold values from -0.5 to 0.5
- w_second: bfloat16 [256, 128], replicated, may hold values from -0.375 to 0.375
- b_second: float32 [128], replicated, may hold values from -1 to 1
Outputs:
- logits: bfloat16 [65536, 128], P(('row', 'col'))
- loss_value: float32 [], replicated
- grad_w_first: float32 [128, 256], replicated
- grad_b_first: float32 [256], replicated
- grad_w_second: float32 [256, 128], replicated
- grad_b_second: float32 [128], replicated
The draws below stay inside these ranges and needn't reach their ends.
Inputs may be any that keep to these rules, and one draw needn't show every extreme that they name: Within one tile the 192 positions (adj_rows, adj_cols) are distinct. Within one tile the 192 positions (adj_rows, adj_cols) are distinct. `adj_live`: some tile has all 192 blocks live.
All inputs are finite; a program needn't handle non-finite values.
Results may differ from the reference program's by a relative error of at most 0.015.
Values may be sent and summed in bfloat16 or wider, within the bound.
A program may use at most 128 MiB of HBM per device.

```python
import jax
import jax.numpy as jnp
from jax import lax

F_IN = 128
HIDDEN_SIZE = 256
CLASSES = 128
BLOCK = 128
NODE_DEV = 256
ROW_BLOCKS = 12
NODES = 65536
BR = 16
BC = 64
KB = 192
N_ROW = 8
N_COL = 32


def block_positions(key):
    tile_keys = jax.random.split(key, N_ROW * N_COL)
    orders = jax.vmap(lambda one_key: jax.random.permutation(one_key, BR * BC))(tile_keys)
    return orders[:, :KB].reshape(N_ROW, N_COL, KB).astype(jnp.int32)


def draw_adj_rows(key, part):
    return (block_positions(key) // BC).astype(jnp.int32)


def draw_adj_cols(key, part):
    return (block_positions(key) % BC).astype(jnp.int32)


def draw_adj_live(key, part):
    key = jax.random.fold_in(key, 7)
    first_key, second_key, third_key = jax.random.split(key, 3)
    first_draw = jax.random.randint(first_key, (N_ROW * N_COL,), 1, KB + 1)
    second_draw = jax.random.randint(second_key, (N_ROW * N_COL,), 1, KB + 1)
    counts = jnp.maximum(first_draw * second_draw // KB, 1)
    chosen = jax.random.randint(third_key, (), 0, N_ROW * N_COL)
    counts = jnp.where(jnp.arange(N_ROW * N_COL) == chosen, KB, counts)
    return counts.reshape(N_ROW, N_COL).astype(jnp.int32)


def draw_train_mask(key, part):
    key = jax.random.fold_in(key, 11)
    positions = jnp.arange(NODES, dtype=jnp.int32)
    threshold = 100 + positions // 64 * 800 // (NODES // 64)
    rolls = jax.random.randint(key, (NODES,), 0, 1000)
    return (rolls < threshold).astype(jnp.int32)


def place_ends(values, key, low, high):
    place = [jax.random.randint(jax.random.fold_in(key, axis), (), 0, length) for axis, length in enumerate(values.shape)]
    main_axis = values.shape.index(max(values.shape))
    beside = place[:main_axis] + [(place[main_axis] + 1) % values.shape[main_axis]] + place[main_axis + 1:]
    return values.at[tuple(place)].set(low).at[tuple(beside)].set(high)


def level_of(key, shape, cuts, smallest, top_value):
    factor_of, own = 1.0, jax.random.fold_in(key, 6)
    for position, parts in cuts:
        heights = jnp.exp(jax.random.uniform(jax.random.fold_in(own, position), (parts,), jnp.float32, smallest / len(cuts), top_value / len(cuts)))
        factor_of = factor_of * jnp.repeat(heights, shape[position] // parts).reshape([-1 if axis == position else 1 for axis in range(len(shape))])
    return factor_of


def gaussian(stream_key, shape, deviation, most, cuts=(), kind=jnp.bfloat16):
    array = deviation * jax.random.normal(stream_key, shape, jnp.float32)
    if cuts:
        array = array * level_of(stream_key, shape, cuts, -0.22, 0.18)
    return jnp.clip(array, -most, most).astype(kind)


def setup_inputs(seed: int = 0) -> dict:
    key_of = jax.random.split(jax.random.key(seed), 12)
    features = gaussian(key_of[0], (NODES, F_IN), 1.0, 6.0, ((0, 256),))
    labels = place_ends(jax.random.randint(key_of[1], (NODES,), 0, CLASSES), jax.random.fold_in(key_of[1], 1), 0, CLASSES - 1).astype(jnp.int32)
    train_mask = draw_train_mask(jax.random.fold_in(key_of[11], 71), 0)
    adj_rows = draw_adj_rows(jax.random.fold_in(key_of[11], 71), 0)
    adj_cols = draw_adj_cols(jax.random.fold_in(key_of[11], 71), 0)
    adj_live = draw_adj_live(jax.random.fold_in(key_of[11], 71), 0)
    adj_values = gaussian(key_of[6], (N_ROW, N_COL, KB, BLOCK, BLOCK), (ROW_BLOCKS * BLOCK * N_COL // 2) ** -0.5, 0.0390625, ((0, 8), (1, 32)))
    w_first = gaussian(key_of[7], (F_IN, HIDDEN_SIZE), F_IN ** -0.5, 0.5)
    b_first = jnp.clip(jax.random.uniform(key_of[8], (HIDDEN_SIZE,), jnp.float32, -0.5, 0.5), -0.5, 0.5)
    w_second = gaussian(key_of[9], (HIDDEN_SIZE, CLASSES), HIDDEN_SIZE ** -0.5, 0.375)
    b_second = jnp.clip(jax.random.uniform(key_of[10], (CLASSES,), jnp.float32, -1.0, 1.0), -1.0, 1.0)
    return {"features": features, "labels": labels, "train_mask": train_mask, "adj_rows": adj_rows, "adj_cols": adj_cols, "adj_live": adj_live, "adj_values": adj_values, "w_first": w_first, "b_first": b_first, "w_second": w_second, "b_second": b_second}


highest = lax.Precision.HIGHEST


def forward_product(adj_rows, adj_cols, adj_live, adj_values, inputs):
    feat_width = inputs.shape[1]
    strips = inputs.astype(jnp.float32).reshape(N_ROW, BC, BLOCK, feat_width)
    totals = jnp.zeros((N_ROW, N_COL, NODE_DEV, feat_width), jnp.float32)

    def tile_step(totals, tile_index):
        grid_row = tile_index // N_COL
        grid_col = tile_index % N_COL
        keep_mask = (jnp.arange(KB, dtype=jnp.int32) < adj_live[grid_row, grid_col]).astype(jnp.float32)
        block_vals = adj_values[grid_row, grid_col].astype(jnp.float32) * keep_mask[:, None, None]
        sources = strips[grid_row][adj_cols[grid_row, grid_col]]
        products = jnp.einsum('kab,kbf->kaf', block_vals, sources, precision=highest)
        onehot = (jnp.arange(BR, dtype=jnp.int32)[:, None] == adj_rows[grid_row, grid_col][None, :]).astype(jnp.float32)
        partial_sum = jnp.einsum('ik,kaf->iaf', onehot, products, precision=highest)
        partial_sum = partial_sum.reshape(N_ROW, NODE_DEV, feat_width)
        totals = totals.at[:, grid_col].add(partial_sum)
        return totals, None

    totals, _ = lax.scan(tile_step, totals, jnp.arange(N_ROW * N_COL, dtype=jnp.int32))
    return totals.reshape(NODES, feat_width)


def backward_product(adj_rows, adj_cols, adj_live, adj_values, inputs):
    feat_width = inputs.shape[1]
    pieces = inputs.astype(jnp.float32).reshape(N_ROW, N_COL, NODE_DEV, feat_width)
    totals = jnp.zeros((N_ROW, N_COL * NODE_DEV, feat_width), jnp.float32)

    def tile_step(totals, tile_index):
        grid_row = tile_index // N_COL
        grid_col = tile_index % N_COL
        keep_mask = (jnp.arange(KB, dtype=jnp.int32) < adj_live[grid_row, grid_col]).astype(jnp.float32)
        block_vals = adj_values[grid_row, grid_col].astype(jnp.float32) * keep_mask[:, None, None]
        row_strip = pieces[:, grid_col].reshape(BR, BLOCK, feat_width)
        sources = row_strip[adj_rows[grid_row, grid_col]]
        products = jnp.einsum('kab,kaf->kbf', block_vals, sources, precision=highest)
        onehot = (jnp.arange(BC, dtype=jnp.int32)[:, None] == adj_cols[grid_row, grid_col][None, :]).astype(jnp.float32)
        partial_sum = jnp.einsum('jk,kbf->jbf', onehot, products, precision=highest)
        partial_sum = partial_sum.reshape(N_COL * NODE_DEV, feat_width)
        totals = totals.at[grid_row].add(partial_sum)
        return totals, None

    totals, _ = lax.scan(tile_step, totals, jnp.arange(N_ROW * N_COL, dtype=jnp.int32))
    return totals.reshape(NODES, feat_width)


def reference(features, labels, train_mask, adj_rows, adj_cols, adj_live, adj_values, w_first, b_first, w_second, b_second):
    agg_in = forward_product(adj_rows, adj_cols, adj_live, adj_values, features)
    pre_hidden = jnp.dot(agg_in, w_first.astype(jnp.float32), precision=highest, preferred_element_type=jnp.float32) + b_first
    hidden = jax.nn.relu(pre_hidden).astype(jnp.bfloat16)
    agg_hidden = forward_product(adj_rows, adj_cols, adj_live, adj_values, hidden)
    scores = jnp.dot(agg_hidden, w_second.astype(jnp.float32), precision=highest, preferred_element_type=jnp.float32) + b_second
    row_max = jnp.max(scores, axis=1, keepdims=True)
    log_total = jnp.log(jnp.sum(jnp.exp(scores - row_max), axis=1, keepdims=True)) + row_max
    onehot = (jnp.arange(CLASSES, dtype=jnp.int32)[None, :] == labels[:, None]).astype(jnp.float32)
    picked = jnp.sum(onehot * scores, axis=1)
    mask_float = train_mask.astype(jnp.float32)
    train_count = jnp.float32(NODES // 2)
    loss_value = jnp.sum(mask_float * (log_total[:, 0] - picked)) / train_count
    d_scores = mask_float[:, None] * (jnp.exp(scores - log_total) - onehot) / train_count
    grad_b_second = jnp.sum(d_scores, axis=0)
    grad_w_second = jnp.dot(agg_hidden.T, d_scores, precision=highest, preferred_element_type=jnp.float32)
    d_agg = jnp.dot(d_scores, w_second.astype(jnp.float32).T, precision=highest, preferred_element_type=jnp.float32)
    d_hidden = backward_product(adj_rows, adj_cols, adj_live, adj_values, d_agg)
    d_pre = jnp.where(pre_hidden > 0, d_hidden, jnp.zeros_like(d_hidden))
    grad_w_first = jnp.dot(agg_in.T, d_pre, precision=highest, preferred_element_type=jnp.float32)
    grad_b_first = jnp.sum(d_pre, axis=0)
    return scores.astype(jnp.bfloat16), loss_value, grad_w_first, grad_b_first, grad_w_second, grad_b_second
```

```python
import functools

import jax
import jax.numpy as jnp
from jax import lax
from jax.experimental import pallas as pl
from jax.experimental.pallas import tpu as pltpu
from jax.sharding import PartitionSpec as P

MESH = pl.DeviceIdType.MESH
F32, BF16 = jnp.float32, jnp.bfloat16
ANY = pl.BlockSpec(memory_space=pl.ANY)
VM = pl.BlockSpec(memory_space=pltpu.VMEM)
SM = pl.BlockSpec(memory_space=pltpu.SMEM)
LIMIT = 40 * 1024 * 1024
UNROLL = 8
GROUP = 16


def dot(a, b):
    return jnp.dot(a, b, preferred_element_type=F32)


def dot_nt(a, b):
    return lax.dot_general(a, b, (((1,), (1,)), ((), ())), preferred_element_type=F32)


def halves(a):
    hi = a.astype(BF16)
    return hi, (a - hi.astype(F32)).astype(BF16)


def place():
    r, c = lax.axis_index("row"), lax.axis_index("col")
    return r, c, c // 4, (c // 2) % 2, c % 2


def remote(src, dst, send, recv, r, c):
    return pltpu.make_async_remote_copy(
        src_ref=src, dst_ref=dst, send_sem=send, recv_sem=recv,
        device_id=(r, c), device_id_type=MESH,
    )


def col_neighbours(z, yl, k):
    up, down = (z + 1) % 8, (z + 7) % 8
    return (4 * up + 2 * yl + k, 4 * down + 2 * yl + k, 4 * z + 2 * (1 - yl) + k, 4 * z + 2 * yl + 1 - k)


def row_peers(r):
    x, yh = r % 4, r // 4
    to, came = [], []
    for dy, dx in ((1, 2), (0, 2), (1, 1), (1, 3), (0, 1), (0, 3), (1, 0)):
        y2 = (yh + dy) % 2
        to.append(4 * y2 + (x + dx) % 4)
        came.append(4 * y2 + (x + 4 - dx) % 4)
    return to, came


def greet(devices):
    barrier = pltpu.get_barrier_semaphore()
    for device in devices:
        pl.semaphore_signal(barrier, inc=1, device_id=device, device_id_type=MESH)
    pl.semaphore_wait(barrier, len(devices))


GATHER_SCRATCH = [
    pltpu.SemaphoreType.DMA((32,)),
    pltpu.SemaphoreType.DMA((32,)),
    pltpu.SemaphoreType.DMA,
]


def gather_col(src, out, send, recv, local):
    r, c, z, yl, k = place()
    up, down, across, twin = col_neighbours(z, yl, k)
    started = []

    def slot_of(dz, other):
        return 4 * ((z + dz + 8) % 8) + 2 * (1 - yl if other else yl) + k

    def push(block, slot, to):
        copy = remote(block, out.at[slot], send.at[len(started)], recv.at[slot], r, to)
        copy.start()
        started.append(copy)

    def arrived(slot):
        remote(src, out.at[slot], send.at[0], recv.at[slot], r, twin).wait_recv()

    for to in (across, up, down, twin):
        push(src, c, to)
    mine = pltpu.make_async_copy(src, out.at[c], local)
    mine.start()
    beside = slot_of(0, True)
    arrived(beside)
    for to in (up, down, twin):
        push(out.at[beside], beside, to)
    for step in range(1, 5):
        for other, rising in ((False, True), (False, False), (True, True), (True, False)):
            reach = 4 if other != rising else 3
            if step > reach:
                continue
            slot = slot_of(-step if rising else step, other)
            arrived(slot)
            if step < reach:
                push(out.at[slot], slot, up if rising else down)
            push(out.at[slot], slot, twin)
    for dz in range(8):
        for other in (False, True):
            far = slot_of(dz, other)
            arrived(far + 1 - 2 * k)
    for copy in started:
        copy.wait_send()
    mine.wait()


def gather_kernel(src, out, send, recv, local):
    r, c, z, yl, k = place()
    greet([(r, n) for n in col_neighbours(z, yl, k)])
    gather_col(src, out, send, recv, local)


def gather_call(features):
    return pl.pallas_call(
        gather_kernel,
        out_shape=jax.ShapeDtypeStruct((32,) + features.shape, BF16),
        in_specs=[ANY],
        out_specs=ANY,
        scratch_shapes=GATHER_SCRATCH,
        compiler_params=pltpu.CompilerParams(collective_id=0, has_side_effects=True, vmem_limit_bytes=LIMIT),
        name="gather_features",
    )(features)


def product_kernel(backward, rows, cols, live, blocks, source, out, held, total, sem):
    n = live[0, 0]
    loads = (n + GROUP - 1) // GROUP

    def load(g):
        part = pl.ds(g * GROUP, GROUP)
        return pltpu.make_async_copy(blocks.at[part], held.at[part], sem.at[g])

    @pl.loop(0, loads)
    def _(g):
        load(g).start()

    outs = total.shape[0] - 1

    @pl.loop(0, outs)
    def _(i):
        total[i] = jnp.zeros(total.shape[1:], F32)

    @pl.loop(0, loads)
    def _(g):
        load(g).wait()
        count = jnp.minimum(n - g * GROUP, GROUP)

        @pl.loop(0, (count + UNROLL - 1) // UNROLL)
        def _(u):
            base = g * GROUP + u * UNROLL
            products, targets = [], []
            for i in range(UNROLL):
                b = base + i
                row, col = rows[0, 0, b], cols[0, 0, b]
                if backward:
                    products.append(dot(source[row], held[b]))
                    targets.append(jnp.where(b < n, col, outs))
                else:
                    products.append(dot(held[b], source[col]))
                    targets.append(jnp.where(b < n, row, outs))
            for product, target in zip(products, targets):
                total[target] += product

    if out.dtype == F32:
        @pl.loop(0, outs)
        def _(i):
            out[i] = total[i]
    else:
        @pl.loop(0, outs)
        def _(i):
            out[i] = total[i].astype(out.dtype)


def product_call(rows, cols, live, blocks, source, outs, dtype, backward, name):
    return pl.pallas_call(
        functools.partial(product_kernel, backward),
        out_shape=jax.ShapeDtypeStruct((outs, 128, 128), dtype),
        in_specs=[SM, SM, SM, ANY, VM],
        out_specs=VM,
        scratch_shapes=[
            pltpu.VMEM(blocks.shape, BF16),
            pltpu.VMEM((outs + 1, 128, 128), F32),
            pltpu.SemaphoreType.DMA((blocks.shape[0] // GROUP,)),
        ],
        compiler_params=pltpu.CompilerParams(vmem_limit_bytes=LIMIT),
        name=name,
    )(rows, cols, live, blocks, source)


def sum_row(parts, inbox, total, send, recv, local):
    r, c, z, yl, k = place()
    to, came = row_peers(r)
    copies = [remote(parts.at[p], inbox.at[r], send.at[i], recv.at[i], p, c) for i, p in enumerate(to)]
    for copy in copies:
        copy.start()
    mine = pltpu.make_async_copy(parts.at[r], inbox.at[r], local)
    mine.start()
    mine.wait()
    total[...] = inbox[r].astype(F32)
    order = (6, 4, 5, 1, 2, 3, 0)
    for i in order:
        remote(parts.at[r], inbox.at[came[i]], send.at[i], recv.at[i], to[i], c).wait_recv()
        total[...] += inbox[came[i]].astype(F32)
    return copies


def first_kernel(parts, w_first, b_first, w_second, strip, hidden_t, mask_t, agg_t,
                 inbox, total, outgoing, send, recv, local, gsend, grecv, glocal):
    r, c, z, yl, k = place()
    to, _ = row_peers(r)
    greet([(p, c) for p in to] + [(r, n) for n in col_neighbours(z, yl, k)])
    copies = sum_row(parts, inbox, total, send, recv, local)
    agg = total[...]
    high, low = halves(agg)
    pre = dot(high, w_first[...]) + dot(low, w_first[...]) + b_first[...]
    hidden = jnp.maximum(pre, 0.0).astype(BF16)
    outgoing[...] = dot(hidden, w_second[...]).astype(BF16)
    hidden_t[...] = hidden.astype(F32).T.astype(BF16)
    mask_t[...] = jnp.where(pre > 0, 1.0, 0.0).T.astype(BF16)
    agg_t[...] = agg.T
    gather_col(outgoing, strip, gsend, grecv, glocal)
    for copy in copies:
        copy.wait_send()


def first_call(parts, w_first, b_first, w_second):
    return pl.pallas_call(
        first_kernel,
        out_shape=(
            jax.ShapeDtypeStruct((32, 256, 128), BF16),
            jax.ShapeDtypeStruct((256, 256), BF16),
            jax.ShapeDtypeStruct((256, 256), BF16),
            jax.ShapeDtypeStruct((128, 256), F32),
        ),
        in_specs=[ANY, VM, VM, VM],
        out_specs=(ANY, VM, VM, VM),
        scratch_shapes=[
            pltpu.VMEM((8, 256, 128), F32),
            pltpu.VMEM((256, 128), F32),
            pltpu.VMEM((256, 128), BF16),
            pltpu.SemaphoreType.DMA((7,)),
            pltpu.SemaphoreType.DMA((7,)),
            pltpu.SemaphoreType.DMA,
        ] + GATHER_SCRATCH,
        compiler_params=pltpu.CompilerParams(collective_id=1, has_side_effects=True, vmem_limit_bytes=LIMIT),
        name="first_layer",
    )(parts, w_first, b_first, w_second)


def second_kernel(parts, labels, train, b_second, logits, stats, grads,
                  inbox, total, outgoing, send, recv, local, gsend, grecv, glocal):
    r, c, z, yl, k = place()
    to, came = row_peers(r)
    greet([(p, c) for p in to])
    copies = sum_row(parts, inbox, total, send, recv, local)
    classes = lax.broadcasted_iota(jnp.int32, (128, 256), 0)
    onehot = jnp.where(classes == labels[...], 1.0, 0.0).T
    mask = jnp.broadcast_to(train[...].astype(F32), (128, 256)).T
    scores = total[...] + b_second[...]
    logits[...] = scores.astype(BF16)
    row_max = jnp.max(scores, axis=1, keepdims=True)
    log_total = jnp.log(jnp.sum(jnp.exp(scores - row_max), axis=1, keepdims=True)) + row_max
    count = 32768.0
    d_scores = mask * (jnp.exp(scores - log_total) - onehot) / count
    for half in range(2):
        outgoing[half] = d_scores[128 * half:128 * half + 128].T.astype(BF16)
    sends = [remote(outgoing, grads.at[r], gsend.at[i], grecv.at[i], p, c) for i, p in enumerate(to)]
    for copy in sends:
        copy.start()
    mine = pltpu.make_async_copy(outgoing, grads.at[r], glocal)
    mine.start()
    cross = mask * onehot * (log_total - scores) / count
    stats[...] = jnp.zeros(stats.shape, F32)
    stats[0:1] = jnp.sum(d_scores, axis=0, keepdims=True)
    stats[1:2] = jnp.sum(cross, axis=0, keepdims=True)
    for i in range(7):
        remote(outgoing, grads.at[came[i]], gsend.at[i], grecv.at[i], to[i], c).wait_recv()
    mine.wait()
    for copy in copies + sends:
        copy.wait_send()


def second_call(parts, labels, train, b_second):
    return pl.pallas_call(
        second_kernel,
        out_shape=(
            jax.ShapeDtypeStruct((256, 128), BF16),
            jax.ShapeDtypeStruct((8, 128), F32),
            jax.ShapeDtypeStruct((8, 2, 128, 128), BF16),
        ),
        in_specs=[ANY, VM, VM, VM],
        out_specs=(VM, VM, ANY),
        scratch_shapes=[
            pltpu.VMEM((8, 256, 128), BF16),
            pltpu.VMEM((256, 128), F32),
            pltpu.VMEM((2, 128, 128), BF16),
        ] + 2 * [
            pltpu.SemaphoreType.DMA((7,)),
            pltpu.SemaphoreType.DMA((7,)),
            pltpu.SemaphoreType.DMA,
        ],
        compiler_params=pltpu.CompilerParams(collective_id=2, has_side_effects=True, vmem_limit_bytes=LIMIT),
        name="second_layer",
    )(parts, labels, train, b_second)


STREAMS = ((True, True, 3), (True, False, 4), (False, True, 4), (False, False, 3))
PIECE = 24


def last_kernel(parts, hidden_t, mask_t, agg_t, w_second, stats,
                g_first, g_second, small,
                twin_box, z_out, z_box, y_out, y_box, grad, pay, box_a, box_b, box_c,
                t_send, t_recv, z_send, z_recv, y_send, y_recv,
                a_send, a_recv, b_send, b_recv, c_send, c_recv):
    r, c, z, yl, k = place()
    up, down, across, twin = col_neighbours(z, yl, k)
    me = 4 * r + c % 4

    def of_plane(j):
        return j // 4, 4 * z + j % 4

    def of_line(j):
        return r, 4 * j + c % 4

    barrier = pltpu.get_barrier_semaphore()

    @pl.loop(1, 32)
    def _(i):
        pl.semaphore_signal(barrier, inc=1, device_id=of_plane((me + i) % 32), device_id_type=MESH)

    @pl.loop(1, 8)
    def _(i):
        pl.semaphore_signal(barrier, inc=1, device_id=of_line((z + i) % 8), device_id_type=MESH)

    pl.semaphore_wait(barrier, 38)

    def twin_copy(zz, row):
        i = 2 * zz + row
        return remote(parts.at[4 * zz + 2 * row + 1 - k], twin_box.at[i], t_send.at[i], t_recv.at[i], r, twin)

    def where(other, dz):
        return (z + dz + 8) % 8, (1 - yl if other else yl)

    order = []
    for step in range(4):
        for other, rising, hops in STREAMS:
            if step < hops:
                order.append(where(other, (hops - step) * (1 if rising else -1)))
    order += [where(True, 0), where(False, 0)]
    for zz, row in order:
        twin_copy(zz, row).start()

    def mine(zz, row):
        twin_copy(zz, row).wait_recv()
        return parts[4 * zz + 2 * row + k].astype(F32) + twin_box[2 * zz + row].astype(F32)

    def z_copy(s, step, rising):
        return remote(z_out.at[s, step], z_box.at[s, step], z_send.at[s, step], z_recv.at[s, step], r, up if rising else down)

    for step in range(4):
        for s, (other, rising, hops) in enumerate(STREAMS):
            if step >= hops:
                continue
            zz, row = where(other, (hops - step) * (1 if rising else -1))
            value = mine(zz, row)
            if step:
                z_copy(s, step - 1, rising).wait_recv()
                value += z_box[s, step - 1].astype(F32)
            z_out[s, step] = value.astype(BF16)
            z_copy(s, step, rising).start()
    value = mine(*where(True, 0))
    for s in (0, 1):
        z_copy(s, STREAMS[s][2] - 1, STREAMS[s][1]).wait_recv()
        value += z_box[s, STREAMS[s][2] - 1].astype(F32)
    y_out[...] = value.astype(BF16)
    y_copy = remote(y_out, y_box, y_send, y_recv, r, across)
    y_copy.start()
    value = mine(*where(False, 0))
    for s in (2, 3):
        z_copy(s, STREAMS[s][2] - 1, STREAMS[s][1]).wait_recv()
        value += z_box[s, STREAMS[s][2] - 1].astype(F32)
    y_copy.wait_recv()
    grad[...] = value + y_box[...].astype(F32)

    g_t = jnp.concatenate([grad[0], grad[1]], axis=1)
    g_hi, g_lo = halves(g_t)
    d_pre = (dot(w_second[...], g_hi) + dot(w_second[...], g_lo)) * mask_t[...].astype(F32)
    d_hi, d_lo = halves(d_pre)
    a_hi, a_lo = halves(agg_t[...])
    first = dot_nt(a_hi, d_hi) + dot_nt(a_lo, d_hi) + dot_nt(a_hi, d_lo)
    second = dot_nt(hidden_t[...], g_hi) + dot_nt(hidden_t[...], g_lo)
    ones = jnp.ones((8, 256), BF16)
    bias = dot_nt(ones, d_hi) + dot_nt(ones, d_lo)
    for p in range(8):
        pay[p, 0:16] = first[16 * p:16 * p + 16, 0:128]
        pay[p + 8, 0:16] = first[16 * p:16 * p + 16, 128:256]
    for p in range(16):
        pay[p + 16, 0:16] = second[16 * p:16 * p + 16]
    for p in range(32):
        pay[p, 16:24] = jnp.zeros((8, 128), F32)
    pay[0, 16:24] = stats[...]
    pay[0, 18:19] = bias[0:1, 0:128]
    pay[0, 19:20] = bias[0:1, 128:256]

    def a_copy(to, frm):
        rr, cc = of_plane(to)
        return remote(pay.at[to], box_a.at[frm], a_send.at[to], a_recv.at[frm], rr, cc)

    def b_copy(to, frm):
        rr, cc = of_line(to)
        return remote(box_b.at[z], box_b.at[frm], b_send.at[to], b_recv.at[frm], rr, cc)

    def c_copy(to, frm):
        rr, cc = of_plane(to)
        return remote(box_c.at[me], box_c.at[frm], c_send.at[to], c_recv.at[frm], rr, cc)

    @pl.loop(1, 32)
    def _(i):
        a_copy((me + i) % 32, me).start()

    def add_a(i, total):
        j = (me + 32 - i) % 32
        a_copy(j, j).wait_recv()
        return total + box_a[j]

    box_b[z] = lax.fori_loop(1, 32, add_a, pay[me])

    @pl.loop(1, 8)
    def _(i):
        b_copy((z + i) % 8, z).start()

    @pl.loop(1, 8)
    def _(i):
        j = (z + i) % 8
        b_copy(j, j).wait_recv()

    total = box_b[0]
    for j in range(1, 8):
        total = total + box_b[j]
    box_c[me] = total

    @pl.loop(1, 32)
    def _(i):
        c_copy((me + i) % 32, me).start()

    @pl.loop(1, 32)
    def _(i):
        j = (me + i) % 32
        c_copy(j, j).wait_recv()

    for p in range(8):
        g_first[16 * p:16 * p + 16, 0:128] = box_c[p, 0:16]
        g_first[16 * p:16 * p + 16, 128:256] = box_c[p + 8, 0:16]
    for p in range(16):
        g_second[16 * p:16 * p + 16] = box_c[p + 16, 0:16]
    tail = box_c[0, 16:24]
    lines = lax.broadcasted_iota(jnp.int32, (8, 128), 0)
    whole = jnp.broadcast_to(jnp.sum(tail, axis=1, keepdims=True), (8, 128))
    small[...] = jnp.where(lines == 1, whole, tail)

    for zz, row in order:
        twin_copy(zz, row).wait_send()
    for s, (other, rising, hops) in enumerate(STREAMS):
        for step in range(hops):
            z_copy(s, step, rising).wait_send()
    y_copy.wait_send()

    @pl.loop(1, 32)
    def _(i):
        j = (me + i) % 32
        a_copy(j, me).wait_send()
        c_copy(j, me).wait_send()

    @pl.loop(1, 8)
    def _(i):
        b_copy((z + i) % 8, z).wait_send()


def last_call(parts, hidden_t, mask_t, agg_t, w_second, stats):
    chunk = (2, 128, 128)
    return pl.pallas_call(
        last_kernel,
        out_shape=(
            jax.ShapeDtypeStruct((128, 256), F32),
            jax.ShapeDtypeStruct((256, 128), F32),
            jax.ShapeDtypeStruct((8, 128), F32),
        ),
        in_specs=[VM] * 6,
        out_specs=(VM, VM, VM),
        scratch_shapes=[
            pltpu.VMEM((16,) + chunk, BF16),
            pltpu.VMEM((4, 4) + chunk, BF16),
            pltpu.VMEM((4, 4) + chunk, BF16),
            pltpu.VMEM(chunk, BF16),
            pltpu.VMEM(chunk, BF16),
            pltpu.VMEM(chunk, F32),
            pltpu.VMEM((32, PIECE, 128), F32),
            pltpu.VMEM((32, PIECE, 128), F32),
            pltpu.VMEM((8, PIECE, 128), F32),
            pltpu.VMEM((32, PIECE, 128), F32),
            pltpu.SemaphoreType.DMA((16,)),
            pltpu.SemaphoreType.DMA((16,)),
            pltpu.SemaphoreType.DMA((4, 4)),
            pltpu.SemaphoreType.DMA((4, 4)),
            pltpu.SemaphoreType.DMA,
            pltpu.SemaphoreType.DMA,
            pltpu.SemaphoreType.DMA((32,)),
            pltpu.SemaphoreType.DMA((32,)),
            pltpu.SemaphoreType.DMA((8,)),
            pltpu.SemaphoreType.DMA((8,)),
            pltpu.SemaphoreType.DMA((32,)),
            pltpu.SemaphoreType.DMA((32,)),
        ],
        compiler_params=pltpu.CompilerParams(collective_id=3, has_side_effects=True, vmem_limit_bytes=LIMIT),
        name="weight_gradients",
    )(parts, hidden_t, mask_t, agg_t, w_second, stats)


def local(features, labels, train_mask, adj_rows, adj_cols, adj_live, adj_values, w_first, b_first, w_second, b_second):
    blocks = adj_values[0, 0]
    product = functools.partial(product_call, adj_rows, adj_cols, adj_live, blocks)
    strip = gather_call(features)
    part = product(strip.reshape(64, 128, 128), 16, F32, False, "product_first")
    strip, hidden_t, mask_t, agg_t = first_call(
        part.reshape(8, 256, 128), w_first, b_first.reshape(1, 256), w_second
    )
    part = product(strip.reshape(64, 128, 128), 16, BF16, False, "product_second")
    logits, stats, grads = second_call(
        part.reshape(8, 256, 128), labels.reshape(1, 256), train_mask.reshape(1, 256), b_second.reshape(1, 128)
    )
    part = product(grads.reshape(16, 128, 128), 64, BF16, True, "product_back")
    g_first, g_second, small = last_call(
        part.reshape(32, 2, 128, 128), hidden_t, mask_t, agg_t, w_second, stats
    )
    return logits, small[1, 0], g_first, small[2:4].reshape(256), g_second, small[0]


def solution(mesh):
    in_specs = (
        P(("row", "col"), None),
        P(("row", "col")),
        P(("row", "col")),
        P("row", "col", None),
        P("row", "col", None),
        P("row", "col"),
        P("row", "col", None, None, None),
        P(),
        P(),
        P(),
        P(),
    )
    out_specs = (P(("row", "col"), None), P(), P(), P(), P(), P())
    return jax.shard_map(local, mesh=mesh, in_specs=in_specs, out_specs=out_specs, check_vma=False)
```

```python
import functools

import jax
import jax.numpy as jnp
from jax import lax
from jax.experimental import pallas as pl
from jax.experimental.pallas import tpu as pltpu
from jax.sharding import PartitionSpec as P

MESH = pl.DeviceIdType.MESH
F32, BF16 = jnp.float32, jnp.bfloat16
ANY = pl.BlockSpec(memory_space=pl.ANY)
VM = pl.BlockSpec(memory_space=pltpu.VMEM)
SM = pl.BlockSpec(memory_space=pltpu.SMEM)
LIMIT = 32 * 1024 * 1024
PRODUCT_LIMIT = 12 * 1024 * 1024
UNROLL = 32
LOADS = 4


def dot(a, b):
    return jnp.dot(a, b, preferred_element_type=F32)


def dot_nt(a, b):
    return lax.dot_general(a, b, (((1,), (1,)), ((), ())), preferred_element_type=F32)


def halves(a):
    hi = a.astype(BF16)
    return hi, (a - hi.astype(F32)).astype(BF16)


def place():
    r, c = lax.axis_index("row"), lax.axis_index("col")
    return r, c, c // 4, (c // 2) % 2, c % 2


def remote(src, dst, send, recv, r, c):
    return pltpu.make_async_remote_copy(
        src_ref=src, dst_ref=dst, send_sem=send, recv_sem=recv,
        device_id=(r, c), device_id_type=MESH,
    )


def col_neighbours(z, yl, k):
    up, down = (z + 1) % 8, (z + 7) % 8
    return (4 * up + 2 * yl + k, 4 * down + 2 * yl + k, 4 * z + 2 * (1 - yl) + k, 4 * z + 2 * yl + 1 - k)


def row_peers(r):
    x, yh = r % 4, r // 4
    to, came = [], []
    for dy, dx in ((1, 2), (0, 2), (1, 1), (1, 3), (0, 1), (0, 3), (1, 0)):
        y2 = (yh + dy) % 2
        to.append(4 * y2 + (x + dx) % 4)
        came.append(4 * y2 + (x + 4 - dx) % 4)
    return to, came


def greet(devices):
    barrier = pltpu.get_barrier_semaphore()
    for device in devices:
        pl.semaphore_signal(barrier, inc=1, device_id=device, device_id_type=MESH)
    pl.semaphore_wait(barrier, len(devices))


def gather_scratch(pieces):
    return [
        pltpu.SemaphoreType.DMA((36 * pieces,)),
        pltpu.SemaphoreType.DMA((32, pieces)),
        pltpu.SemaphoreType.DMA((pieces,)),
    ]


class Gather:
    STAGES = (
        ((-1, False, "ut"), (1, False, "dt"), (0, True, "udt")),
        ((-2, False, "uat"), (2, False, "dt"), (1, True, "dt"), (-1, True, "t")),
        ((-3, False, "uat"), (3, False, "at"), (2, True, "t"), (-2, True, "t")),
        ((-4, False, "at"), (-3, True, "t"), (3, True, "t")),
        ((-4, True, "t"),),
    )

    def __init__(self, src, out, pieces, send, recv, local):
        self.src, self.out, self.pieces, self.send, self.recv, self.local = src, out, pieces, send, recv, local
        self.rows = src.shape[0] // pieces
        self.r, self.c, self.z, self.yl, self.k = place()
        up, down, across, twin = col_neighbours(self.z, self.yl, self.k)
        self.to = {"u": up, "d": down, "a": across, "t": twin}
        self.started, self.kept = [], []

    def slot(self, dz, other):
        return 4 * ((self.z + dz + 8) % 8) + 2 * (1 - self.yl if other else self.yl) + self.k

    def part(self, slot, s):
        return self.out.at[slot, pl.ds(s * self.rows, self.rows)]

    def push(self, block, slot, s, targets):
        for name in targets:
            copy = remote(block, self.part(slot, s), self.send.at[len(self.started)], self.recv.at[slot, s], self.r, self.to[name])
            copy.start()
            self.started.append(copy)

    def arrived(self, slot, s):
        block = self.part(slot, s)
        remote(block, block, self.send.at[0], self.recv.at[slot, s], self.r, self.to["t"]).wait_recv()

    def begin(self, s):
        block = self.src.at[pl.ds(s * self.rows, self.rows)]
        self.push(block, self.c, s, "udat")
        mine = pltpu.make_async_copy(block, self.part(self.c, s), self.local.at[s])
        mine.start()
        self.kept.append(mine)

    def stage(self, n, s):
        for dz, other, targets in self.STAGES[n - 1]:
            slot = self.slot(dz, other)
            self.arrived(slot, s)
            self.push(self.part(slot, s), slot, s, targets)

    def end(self):
        for s in range(self.pieces):
            for dz in range(8):
                for other in (False, True):
                    self.arrived(self.slot(dz, other) + 1 - 2 * self.k, s)
        for copy in self.kept:
            copy.wait()
        for copy in self.started:
            copy.wait_send()


def gather_kernel(src, blocks, out, held, load_sem, *sems):
    r, c, z, yl, k = place()
    greet([(r, n) for n in col_neighbours(z, yl, k)])
    gather = Gather(src, out, 1, *sems)
    gather.begin(0)
    share = blocks.shape[0] // LOADS
    loads = [
        pltpu.make_async_copy(blocks.at[pl.ds(i * share, share)], held.at[pl.ds(i * share, share)], load_sem.at[i])
        for i in range(LOADS)
    ]
    for load in loads:
        load.start()
    for n in range(1, 6):
        gather.stage(n, 0)
    gather.end()
    for load in loads:
        load.wait()


def gather_call(features, blocks):
    return pl.pallas_call(
        gather_kernel,
        out_shape=(
            jax.ShapeDtypeStruct((32,) + features.shape, BF16),
            jax.ShapeDtypeStruct(blocks.shape, BF16),
        ),
        in_specs=[ANY, ANY],
        out_specs=(VM, VM),
        scratch_shapes=[pltpu.SemaphoreType.DMA((LOADS,))] + gather_scratch(1),
        compiler_params=pltpu.CompilerParams(collective_id=0, has_side_effects=True, vmem_limit_bytes=LIMIT),
        name="gather_features",
    )(pltpu.with_memory_space_constraint(features, pltpu.HBM), pltpu.with_memory_space_constraint(blocks, pltpu.HBM))


def product_kernel(backward, rows, cols, live, blocks, source, out, total):
    n = live[0, 0]
    outs = total.shape[0] - 1

    @pl.loop(0, outs, unroll=2)
    def _(i):
        total[i] = jnp.zeros(total.shape[1:], F32)

    @pl.loop(0, (n + UNROLL - 1) // UNROLL)
    def _(u):
        products, targets = [], []
        for i in range(UNROLL):
            b = u * UNROLL + i
            row, col = rows[0, 0, b], cols[0, 0, b]
            if backward:
                products.append(dot(source[row], blocks[b]))
                targets.append(jnp.where(b < n, col, outs))
            else:
                products.append(dot(blocks[b], source[col]))
                targets.append(jnp.where(b < n, row, outs))
        for product, target in zip(products, targets):
            total[target] += product

    @pl.loop(0, outs, unroll=2)
    def _(i):
        out[i] = total[i].astype(out.dtype)


def product_call(rows, cols, live, blocks, source, outs, dtype, backward, name):
    return pl.pallas_call(
        functools.partial(product_kernel, backward),
        out_shape=jax.ShapeDtypeStruct((outs, 128, 128), dtype),
        in_specs=[SM, SM, SM, VM, VM],
        out_specs=VM,
        scratch_shapes=[pltpu.VMEM((outs + 1, 128, 128), F32)],
        compiler_params=pltpu.CompilerParams(vmem_limit_bytes=PRODUCT_LIMIT),
        name=name,
    )(rows, cols, live, blocks, source)


class RowSum:
    def __init__(self, parts, inbox, pieces, send, recv, local):
        self.parts, self.inbox, self.send, self.recv, self.local = parts, inbox, send, recv, local
        self.rows = inbox.shape[1] // pieces
        self.r, self.c, _, _, _ = place()
        self.to, self.came = row_peers(self.r)
        self.copies, self.mine = [], []
        for s in range(pieces):
            for i in range(7):
                self.copies.append(self.copy(i, self.r, s))
                self.copies[-1].start()
            part = pl.ds(s * self.rows, self.rows)
            self.mine.append(pltpu.make_async_copy(parts.at[self.r, part], inbox.at[self.r, part], local.at[s]))
            self.mine[-1].start()

    def copy(self, i, slot, s):
        part = pl.ds(s * self.rows, self.rows)
        return remote(self.parts.at[self.to[i], part], self.inbox.at[slot, part], self.send.at[i, s], self.recv.at[i, s], self.to[i], self.c)

    def piece(self, s):
        part = slice(s * self.rows, (s + 1) * self.rows)
        self.mine[s].wait()
        total = self.inbox[self.r, part].astype(F32)
        for i in (6, 4, 5, 1, 2, 3, 0):
            self.copy(i, self.came[i], s).wait_recv()
            total = total + self.inbox[self.came[i], part].astype(F32)
        return total

    def end(self):
        for copy in self.copies:
            copy.wait_send()


def first_kernel(parts, w_first, b_first, w_second, strip, hidden_t, mask_t, agg_t,
                 inbox, outgoing, send, recv, local, gsend, grecv, glocal):
    r, c, z, yl, k = place()
    to, _ = row_peers(r)
    greet([(p, c) for p in to] + [(r, n) for n in col_neighbours(z, yl, k)])
    row_sum = RowSum(parts, inbox, 1, send, recv, local)
    gather = Gather(outgoing, strip, 1, gsend, grecv, glocal)

    def begin(s):
        agg = row_sum.piece(s)
        high, low = halves(agg)
        pre = dot(high, w_first[...]) + dot(low, w_first[...]) + b_first[...]
        hidden = jnp.maximum(pre, 0.0).astype(BF16)
        part = slice(0, 256)
        outgoing[part] = dot(hidden, w_second[...]).astype(BF16)
        gather.begin(s)
        hidden_t[:, part] = hidden.astype(F32).T.astype(BF16)
        mask_t[:, part] = jnp.where(pre > 0, 1.0, 0.0).T.astype(BF16)
        agg_t[:, part] = agg.T

    begin(0)
    for n in range(1, 6):
        gather.stage(n, 0)
    gather.end()
    row_sum.end()


def first_call(parts, w_first, b_first, w_second):
    return pl.pallas_call(
        first_kernel,
        out_shape=(
            jax.ShapeDtypeStruct((32, 256, 128), BF16),
            jax.ShapeDtypeStruct((256, 256), BF16),
            jax.ShapeDtypeStruct((256, 256), BF16),
            jax.ShapeDtypeStruct((128, 256), F32),
        ),
        in_specs=[ANY, VM, VM, VM],
        out_specs=(VM, VM, VM, VM),
        scratch_shapes=[
            pltpu.VMEM((8, 256, 128), F32),
            pltpu.VMEM((256, 128), BF16),
            pltpu.SemaphoreType.DMA((7, 2)),
            pltpu.SemaphoreType.DMA((7, 2)),
            pltpu.SemaphoreType.DMA((2,)),
        ] + gather_scratch(2),
        compiler_params=pltpu.CompilerParams(collective_id=1, has_side_effects=True, vmem_limit_bytes=LIMIT),
        name="first_layer",
    )(parts, w_first, b_first, w_second)


def second_kernel(parts, labels, train, b_second, logits, stats, grads,
                  inbox, outgoing, send, recv, local, gsend, grecv, glocal):
    r, c, z, yl, k = place()
    to, came = row_peers(r)
    greet([(p, c) for p in to])
    row_sum = RowSum(parts, inbox, 2, send, recv, local)
    classes = lax.broadcasted_iota(jnp.int32, (128, 256), 0)
    onehot = jnp.where(classes == labels[...], 1.0, 0.0).T
    mask = jnp.broadcast_to(train[...].astype(F32), (128, 256)).T
    count = 32768.0
    sends, mine = [], []
    stats[...] = jnp.zeros(stats.shape, F32)

    def grad_copy(i, slot, s):
        return remote(outgoing.at[s], grads.at[slot, s], gsend.at[i, s], grecv.at[i, s], to[i], c)

    for s in range(2):
        part = slice(128 * s, 128 * s + 128)
        scores = row_sum.piece(s) + b_second[...]
        row_max = jnp.max(scores, axis=1, keepdims=True)
        log_total = jnp.log(jnp.sum(jnp.exp(scores - row_max), axis=1, keepdims=True)) + row_max
        d_scores = mask[part] * (jnp.exp(scores - log_total) - onehot[part]) / count
        outgoing[s] = d_scores.T.astype(BF16)
        for i in range(7):
            sends.append(grad_copy(i, r, s))
            sends[-1].start()
        mine.append(pltpu.make_async_copy(outgoing.at[s], grads.at[r, s], glocal.at[s]))
        mine[-1].start()
        logits[part] = scores.astype(BF16)
        cross = mask[part] * onehot[part] * (log_total - scores) / count
        stats[0:1] += jnp.sum(d_scores, axis=0, keepdims=True)
        stats[1:2] += jnp.sum(cross, axis=0, keepdims=True)
    for s in range(2):
        for i in range(7):
            grad_copy(i, came[i], s).wait_recv()
        mine[s].wait()
    row_sum.end()
    for copy in sends:
        copy.wait_send()


def second_call(parts, labels, train, b_second):
    return pl.pallas_call(
        second_kernel,
        out_shape=(
            jax.ShapeDtypeStruct((256, 128), BF16),
            jax.ShapeDtypeStruct((8, 128), F32),
            jax.ShapeDtypeStruct((8, 2, 128, 128), BF16),
        ),
        in_specs=[ANY, VM, VM, VM],
        out_specs=(VM, VM, VM),
        scratch_shapes=[
            pltpu.VMEM((8, 256, 128), BF16),
            pltpu.VMEM((2, 128, 128), BF16),
        ] + 2 * [
            pltpu.SemaphoreType.DMA((7, 2)),
            pltpu.SemaphoreType.DMA((7, 2)),
            pltpu.SemaphoreType.DMA((2,)),
        ],
        compiler_params=pltpu.CompilerParams(collective_id=2, has_side_effects=True, vmem_limit_bytes=LIMIT),
        name="second_layer",
    )(parts, labels, train, b_second)


STREAMS = ((True, True, 3), (True, False, 4), (False, True, 4), (False, False, 3))
PIECE = 24


def last_kernel(parts, hidden_t, mask_t, agg_t, w_second, stats,
                sums,
                twin_box, z_out, z_box, y_out, y_box, grad, pay, box_t, half, box_x, quarter, box_y, box_z,
                t_send, t_recv, z_send, z_recv, y_send, y_recv,
                a_send, a_recv, b_send, b_recv, c_send, c_recv):
    r, c, z, yl, k = place()
    up, down, across, twin = col_neighbours(z, yl, k)
    x, y = r % 4, 2 * (r // 4) + yl

    def on_x(j):
        return r - x + j, c

    def on_y(j):
        return 4 * (j // 2) + x, 4 * z + 2 * (j % 2) + k

    def on_z(j):
        return r, 4 * j + 2 * yl + k

    greet([on_x((x + i) % 4) for i in (1, 2, 3)] + [on_y((y + i) % 4) for i in (1, 2, 3)]
          + [on_z((z + i) % 8) for i in range(1, 8)] + [(r, twin)])

    def twin_copy(zz, row):
        i = 2 * zz + row
        return remote(parts.at[4 * zz + 2 * row + 1 - k], twin_box.at[i], t_send.at[i], t_recv.at[i], r, twin)

    def where(other, dz):
        return (z + dz + 8) % 8, (1 - yl if other else yl)

    order = []
    for step in range(4):
        for other, rising, hops in STREAMS:
            if step < hops:
                order.append(where(other, (hops - step) * (1 if rising else -1)))
    order += [where(True, 0), where(False, 0)]
    for zz, row in order:
        twin_copy(zz, row).start()

    def mine(zz, row):
        twin_copy(zz, row).wait_recv()
        return parts[4 * zz + 2 * row + k].astype(F32) + twin_box[2 * zz + row].astype(F32)

    def z_copy(s, step, rising):
        return remote(z_out.at[s, step], z_box.at[s, step], z_send.at[s, step], z_recv.at[s, step], r, up if rising else down)

    for step in range(4):
        for s, (other, rising, hops) in enumerate(STREAMS):
            if step >= hops:
                continue
            zz, row = where(other, (hops - step) * (1 if rising else -1))
            value = mine(zz, row)
            if step:
                z_copy(s, step - 1, rising).wait_recv()
                value += z_box[s, step - 1].astype(F32)
            z_out[s, step] = value.astype(BF16)
            z_copy(s, step, rising).start()
    value = mine(*where(True, 0))
    for s in (0, 1):
        z_copy(s, STREAMS[s][2] - 1, STREAMS[s][1]).wait_recv()
        value += z_box[s, STREAMS[s][2] - 1].astype(F32)
    y_out[...] = value.astype(BF16)
    y_copy = remote(y_out, y_box, y_send, y_recv, r, across)
    y_copy.start()
    value = mine(*where(False, 0))
    for s in (2, 3):
        z_copy(s, STREAMS[s][2] - 1, STREAMS[s][1]).wait_recv()
        value += z_box[s, STREAMS[s][2] - 1].astype(F32)
    y_copy.wait_recv()
    grad[...] = value + y_box[...].astype(F32)

    g_t = jnp.concatenate([grad[0], grad[1]], axis=1)
    g_hi, g_lo = halves(g_t)
    d_pre = (dot(w_second[...], g_hi) + dot(w_second[...], g_lo)) * mask_t[...].astype(F32)
    d_hi, d_lo = halves(d_pre)
    a_hi, a_lo = halves(agg_t[...])
    first = dot_nt(a_hi, d_hi) + dot_nt(a_lo, d_hi) + dot_nt(a_hi, d_lo)
    second = dot_nt(hidden_t[...], g_hi) + dot_nt(hidden_t[...], g_lo)
    ones = jnp.ones((8, 256), BF16)
    bias = dot_nt(ones, d_hi) + dot_nt(ones, d_lo)
    for p in range(8):
        pay[p, 0:16] = first[16 * p:16 * p + 16, 0:128]
        pay[p + 8, 0:16] = first[16 * p:16 * p + 16, 128:256]
    for p in range(16):
        pay[p + 16, 0:16] = second[16 * p:16 * p + 16]
    for p in range(32):
        pay[p, 16:24] = jnp.zeros((8, 128), F32)
    pay[0, 16:24] = stats[...]
    pay[0, 18:19] = bias[0:1, 0:128]
    pay[0, 19:20] = bias[0:1, 128:256]

    mine16, mine4, p = 16 * k, 16 * k + 4 * x, 16 * k + 4 * x + y
    half_copy = remote(pay.at[pl.ds(16 - mine16, 16)], box_t, a_send.at[0], a_recv.at[0], r, twin)
    half_copy.start()
    half_copy.wait_recv()
    half[...] = pay[pl.ds(mine16, 16)] + box_t[...]

    def x_copy(j, frm):
        return remote(half.at[pl.ds(4 * j, 4)], box_x.at[frm], b_send.at[0, j], b_recv.at[0, frm], *on_x(j))

    def y_part(j, frm):
        return remote(quarter.at[j], box_y.at[frm], b_send.at[1, j], b_recv.at[1, frm], *on_y(j))

    def z_part(j, frm):
        return remote(box_z.at[z], box_z.at[frm], c_send.at[j], c_recv.at[frm], *on_z(j))

    def y_back(j, frm):
        block = sums.at[mine4 + frm]
        return remote(block, block, b_send.at[2, j], b_recv.at[2, frm], *on_y(j))

    def x_back(j, frm):
        block = sums.at[pl.ds(mine16 + 4 * frm, 4)]
        return remote(block, block, b_send.at[3, j], b_recv.at[3, frm], *on_x(j))

    xs, ys, zs = [(x + i) % 4 for i in (2, 1, 3)], [(y + i) % 4 for i in (2, 1, 3)], [(z + i) % 8 for i in (4, 3, 5, 2, 6, 1, 7)]

    def exchange(copy, peers, me):
        for j in peers:
            copy(j, me).start()
        for j in reversed(peers):
            copy(j, j).wait_recv()

    exchange(x_copy, xs, x)
    total = half[pl.ds(4 * x, 4)]
    for j in xs:
        total = total + box_x[j]
    quarter[...] = total
    exchange(y_part, ys, y)
    total = quarter[y]
    for j in ys:
        total = total + box_y[j]
    box_z[z] = total
    exchange(z_part, zs, z)
    total = box_z[0]
    for j in range(1, 8):
        total = total + box_z[j]
    sums[p] = total
    exchange(y_back, ys, y)
    exchange(x_back, xs, x)
    back = sums.at[pl.ds(mine16, 16)]
    back_copy = remote(back, back, a_send.at[1], a_recv.at[1], r, twin)
    back_copy.start()
    other_half = sums.at[pl.ds(16 - mine16, 16)]
    remote(other_half, other_half, a_send.at[1], a_recv.at[1], r, twin).wait_recv()

    for zz, row in order:
        twin_copy(zz, row).wait_send()
    for s, (other, rising, hops) in enumerate(STREAMS):
        for step in range(hops):
            z_copy(s, step, rising).wait_send()
    y_copy.wait_send()
    half_copy.wait_send()
    back_copy.wait_send()
    for copy, peers, me in ((x_copy, xs, x), (y_part, ys, y), (z_part, zs, z), (y_back, ys, y), (x_back, xs, x)):
        for j in peers:
            copy(j, me).wait_send()


def last_call(parts, hidden_t, mask_t, agg_t, w_second, stats):
    chunk = (2, 128, 128)
    return pl.pallas_call(
        last_kernel,
        out_shape=jax.ShapeDtypeStruct((32, PIECE, 128), F32),
        in_specs=[VM] * 6,
        out_specs=VM,
        scratch_shapes=[
            pltpu.VMEM((16,) + chunk, BF16),
            pltpu.VMEM((4, 4) + chunk, BF16),
            pltpu.VMEM((4, 4) + chunk, BF16),
            pltpu.VMEM(chunk, BF16),
            pltpu.VMEM(chunk, BF16),
            pltpu.VMEM(chunk, F32),
            pltpu.VMEM((32, PIECE, 128), F32),
            pltpu.VMEM((16, PIECE, 128), F32),
            pltpu.VMEM((16, PIECE, 128), F32),
            pltpu.VMEM((4, 4, PIECE, 128), F32),
            pltpu.VMEM((4, PIECE, 128), F32),
            pltpu.VMEM((4, PIECE, 128), F32),
            pltpu.VMEM((8, PIECE, 128), F32),
            pltpu.SemaphoreType.DMA((16,)),
            pltpu.SemaphoreType.DMA((16,)),
            pltpu.SemaphoreType.DMA((4, 4)),
            pltpu.SemaphoreType.DMA((4, 4)),
            pltpu.SemaphoreType.DMA,
            pltpu.SemaphoreType.DMA,
            pltpu.SemaphoreType.DMA((2,)),
            pltpu.SemaphoreType.DMA((2,)),
            pltpu.SemaphoreType.DMA((4, 4)),
            pltpu.SemaphoreType.DMA((4, 4)),
            pltpu.SemaphoreType.DMA((8,)),
            pltpu.SemaphoreType.DMA((8,)),
        ],
        compiler_params=pltpu.CompilerParams(collective_id=3, has_side_effects=True, vmem_limit_bytes=LIMIT),
        name="weight_gradients",
    )(parts, hidden_t, mask_t, agg_t, w_second, stats)


def finish_kernel(sums, scores, logits, loss, g_first, b_first, g_second, b_second):
    logits[...] = scores[...]
    for p in range(8):
        g_first[16 * p:16 * p + 16, 0:128] = sums[p, 0:16]
        g_first[16 * p:16 * p + 16, 128:256] = sums[p + 8, 0:16]
    for p in range(16):
        g_second[16 * p:16 * p + 16] = sums[p + 16, 0:16]
    b_second[...] = sums[0, 16:17]
    loss[...] = jnp.sum(sums[0, 17:18], axis=1, keepdims=True)
    b_first[:, 0:128] = sums[0, 18:19]
    b_first[:, 128:256] = sums[0, 19:20]


def finish_call(sums, scores):
    return pl.pallas_call(
        finish_kernel,
        out_shape=(
            jax.ShapeDtypeStruct((256, 128), BF16),
            jax.ShapeDtypeStruct((1, 1), F32),
            jax.ShapeDtypeStruct((128, 256), F32),
            jax.ShapeDtypeStruct((1, 256), F32),
            jax.ShapeDtypeStruct((256, 128), F32),
            jax.ShapeDtypeStruct((1, 128), F32),
        ),
        in_specs=[VM, VM],
        out_specs=(VM,) * 6,
        compiler_params=pltpu.CompilerParams(vmem_limit_bytes=4 * 1024 * 1024),
        name="outputs",
    )(sums, scores)


def local(features, labels, train_mask, adj_rows, adj_cols, adj_live, adj_values, w_first, b_first, w_second, b_second):
    strip, blocks = gather_call(features, adj_values[0, 0])
    product = functools.partial(product_call, adj_rows, adj_cols, adj_live, blocks)
    part = product(strip.reshape(64, 128, 128), 16, F32, False, "product_first")
    strip, hidden_t, mask_t, agg_t = first_call(
        part.reshape(8, 256, 128), w_first, b_first.reshape(1, 256), w_second
    )
    part = product(strip.reshape(64, 128, 128), 16, BF16, False, "product_second")
    scores, stats, grads = second_call(
        part.reshape(8, 256, 128), labels.reshape(1, 256), train_mask.reshape(1, 256), b_second.reshape(1, 128)
    )
    part = product(grads.reshape(16, 128, 128), 64, BF16, True, "product_back")
    sums = last_call(part.reshape(32, 2, 128, 128), hidden_t, mask_t, agg_t, w_second, stats)
    logits, loss, g_first, gb_first, g_second, gb_second = finish_call(sums, scores)
    return logits, loss.reshape(()), g_first, gb_first.reshape(256), g_second, gb_second.reshape(128)


def solution(mesh):
    in_specs = (
        P(("row", "col"), None),
        P(("row", "col")),
        P(("row", "col")),
        P("row", "col", None),
        P("row", "col", None),
        P("row", "col"),
        P("row", "col", None, None, None),
        P(),
        P(),
        P(),
        P(),
    )
    out_specs = (P(("row", "col"), None), P(), P(), P(), P(), P())
    return jax.shard_map(local, mesh=mesh, in_specs=in_specs, out_specs=out_specs, check_vma=False)
```

```python
import functools

import jax
import jax.numpy as jnp
from jax import lax
from jax.experimental import pallas as pl
from jax.experimental.pallas import tpu as pltpu
from jax.sharding import PartitionSpec as P

MESH = pl.DeviceIdType.MESH
F32, BF16 = jnp.float32, jnp.bfloat16
ANY = pl.BlockSpec(memory_space=pl.ANY)
VM = pl.BlockSpec(memory_space=pltpu.VMEM)
SM = pl.BlockSpec(memory_space=pltpu.SMEM)
LIMIT = 32 * 1024 * 1024
PRODUCT_LIMIT = 24 * 1024 * 1024
UNROLL = 32
STEP = 2048
PIECES, STAGGER = 2, False
ORDER = tuple((n, s) for n in range(6) for s in range(2))
LOADS = 4


def dot(a, b):
    return jnp.dot(a, b, preferred_element_type=F32)


def dot_tn(a, b):
    return lax.dot_general(a, b, (((0,), (0,)), ((), ())), preferred_element_type=F32)


def halves(a):
    hi = a.astype(BF16)
    return hi, (a - hi.astype(F32)).astype(BF16)


def place():
    r, c = lax.axis_index("row"), lax.axis_index("col")
    return r, c, c // 4, (c // 2) % 2, c % 2


def remote(src, dst, send, recv, r, c):
    return pltpu.make_async_remote_copy(
        src_ref=src, dst_ref=dst, send_sem=send, recv_sem=recv,
        device_id=(r, c), device_id_type=MESH,
    )


def col_neighbours(z, yl, k):
    up, down = (z + 1) % 8, (z + 7) % 8
    return (4 * up + 2 * yl + k, 4 * down + 2 * yl + k, 4 * z + 2 * (1 - yl) + k, 4 * z + 2 * yl + 1 - k)


def row_peers(r):
    x, yh = r % 4, r // 4
    to, came = [], []
    for dy, dx in ((1, 2), (0, 2), (1, 1), (1, 3), (0, 1), (0, 3), (1, 0)):
        y2 = (yh + dy) % 2
        to.append(4 * y2 + (x + dx) % 4)
        came.append(4 * y2 + (x + 4 - dx) % 4)
    return to, came


def greet(devices):
    barrier = pltpu.get_barrier_semaphore()
    for device in devices:
        pl.semaphore_signal(barrier, inc=1, device_id=device, device_id_type=MESH)
    pl.semaphore_wait(barrier, len(devices))


def gather_scratch(pieces):
    return [
        pltpu.SemaphoreType.DMA((36 * pieces,)),
        pltpu.SemaphoreType.DMA((32, pieces)),
        pltpu.SemaphoreType.DMA((pieces,)),
    ]


class Gather:
    STAGES = (
        ((-1, False, "ut"), (1, False, "dt"), (0, True, "udt")),
        ((-2, False, "uat"), (2, False, "dt"), (1, True, "dt"), (-1, True, "t")),
        ((-3, False, "uat"), (3, False, "at"), (2, True, "t"), (-2, True, "t")),
        ((-4, False, "at"), (-3, True, "t"), (3, True, "t")),
        ((-4, True, "t"),),
    )

    def __init__(self, src, out, pieces, send, recv, local):
        self.src, self.out, self.pieces, self.send, self.recv, self.local = src, out, pieces, send, recv, local
        self.rows = src.shape[0] // pieces
        self.r, self.c, self.z, self.yl, self.k = place()
        up, down, across, twin = col_neighbours(self.z, self.yl, self.k)
        self.to = {"u": up, "d": down, "a": across, "t": twin}
        self.started, self.kept = [], []

    def slot(self, dz, other):
        return 4 * ((self.z + dz + 8) % 8) + 2 * (1 - self.yl if other else self.yl) + self.k

    def part(self, slot, s):
        return self.out.at[slot, pl.ds(s * self.rows, self.rows)]

    def push(self, block, slot, s, targets):
        for name in targets:
            copy = remote(block, self.part(slot, s), self.send.at[len(self.started)], self.recv.at[slot, s], self.r, self.to[name])
            copy.start()
            self.started.append(copy)

    def arrived(self, slot, s):
        block = self.part(slot, s)
        remote(block, block, self.send.at[0], self.recv.at[slot, s], self.r, self.to["t"]).wait_recv()

    def begin(self, s):
        block = self.src.at[pl.ds(s * self.rows, self.rows)]
        self.push(block, self.c, s, "udat")
        mine = pltpu.make_async_copy(block, self.part(self.c, s), self.local.at[s])
        mine.start()
        self.kept.append(mine)

    def stage(self, n, s):
        for dz, other, targets in self.STAGES[n - 1]:
            slot = self.slot(dz, other)
            self.arrived(slot, s)
            self.push(self.part(slot, s), slot, s, targets)

    def end(self):
        for s in range(self.pieces):
            for dz in range(8):
                for other in (False, True):
                    self.arrived(self.slot(dz, other) + 1 - 2 * self.k, s)
        for copy in self.kept:
            copy.wait()
        for copy in self.started:
            copy.wait_send()


def gather_kernel(src, blocks, out, held, load_sem, *sems):
    r, c, z, yl, k = place()
    greet([(r, n) for n in col_neighbours(z, yl, k)])
    gather = Gather(src, out, 1, *sems)
    gather.begin(0)
    share = blocks.shape[0] // LOADS
    loads = [
        pltpu.make_async_copy(blocks.at[pl.ds(i * share, share)], held.at[pl.ds(i * share, share)], load_sem.at[i])
        for i in range(LOADS)
    ]
    for load in loads:
        load.start()
    for n in range(1, 6):
        gather.stage(n, 0)
    gather.end()
    for load in loads:
        load.wait()


def gather_call(features, blocks):
    return pl.pallas_call(
        gather_kernel,
        out_shape=(
            jax.ShapeDtypeStruct((32,) + features.shape, BF16),
            jax.ShapeDtypeStruct(blocks.shape, BF16),
        ),
        in_specs=[ANY, ANY],
        out_specs=(VM, VM),
        scratch_shapes=[pltpu.SemaphoreType.DMA((LOADS,))] + gather_scratch(1),
        compiler_params=pltpu.CompilerParams(collective_id=0, has_side_effects=True, vmem_limit_bytes=LIMIT),
        name="gather_features",
    )(pltpu.with_memory_space_constraint(features, pltpu.HBM), pltpu.with_memory_space_constraint(blocks, pltpu.HBM))


def sparse_product(backward, rows, cols, live, blocks, source, total):
    n = jnp.max(live[...])
    outs = total.shape[0] - 1

    @pl.loop(0, outs, unroll=2)
    def _(i):
        total[i] = jnp.zeros(total.shape[1:], F32)

    @pl.loop(0, (n + UNROLL - 1) // UNROLL)
    def _(u):
        products, targets = [], []
        for i in range(UNROLL):
            b = u * UNROLL + i
            row, col = rows[0, 0, b], cols[0, 0, b]
            if backward:
                products.append(dot_tn(blocks[b], source[row]))
                targets.append(jnp.where(b < n, col, outs))
            else:
                products.append(dot(blocks[b], source[col]))
                targets.append(jnp.where(b < n, row, outs))
        for product, target in zip(products, targets):
            total[target] += product


def product_first_kernel(rows, cols, live, blocks, source, out, total):
    sparse_product(False, rows, cols, live, blocks, source, total)

    @pl.loop(0, out.shape[0], unroll=2)
    def _(i):
        out[i] = total[i]


def product_second_kernel(rows, cols, live, blocks, agg, w_first, b_first, w_second, out, hidden, source, total):
    nodes = STEP // 128

    @pl.loop(0, source.shape[0] // nodes)
    def _(i):
        part = pl.ds(i * nodes, nodes)
        high, low = halves(agg[part].reshape(STEP, 128))
        pre = dot(high, w_first[...]) + dot(low, w_first[...]) + b_first[...]
        kept = jnp.maximum(pre, 0.0).astype(BF16)
        hidden[part] = kept.reshape(nodes, 128, 256)
        source[part] = dot(kept, w_second[...]).astype(BF16).reshape(nodes, 128, 128)

    sparse_product(False, rows, cols, live, blocks, source, total)

    @pl.loop(0, out.shape[0], unroll=2)
    def _(i):
        out[i] = total[i].astype(BF16)


def product_back_kernel(rows, cols, live, blocks, source, agg, hidden, w_second, stats, pay,
                        total, g_first, g_second, g_bias):
    sparse_product(True, rows, cols, live, blocks, source, total)
    nodes = STEP // 128
    w_second_t = w_second[...].astype(F32).T.astype(BF16)
    g_first[...] = jnp.zeros(g_first.shape, F32)
    g_second[...] = jnp.zeros(g_second.shape, F32)
    g_bias[...] = jnp.zeros(g_bias.shape, F32)

    @pl.loop(0, hidden.shape[0] // nodes)
    def _(i):
        part = pl.ds(i * nodes, nodes)
        grad = total[part].reshape(STEP, 128).astype(BF16)
        kept = hidden[part].reshape(STEP, 256)
        d_pre = jnp.where(kept > 0, dot(grad, w_second_t), 0.0)
        g_second[...] += dot_tn(kept, grad)
        g_first[...] += dot_tn(agg[part].reshape(STEP, 128).astype(BF16), d_pre.astype(BF16))
        g_bias[...] += jnp.sum(d_pre.reshape(STEP // 8, 8, 256), axis=0)

    for p in range(8):
        pay[p, 0:16] = g_first[16 * p:16 * p + 16, 0:128]
        pay[p + 8, 0:16] = g_first[16 * p:16 * p + 16, 128:256]
    for p in range(16):
        pay[p + 16, 0:16] = g_second[16 * p:16 * p + 16]
    for p in range(4, 32):
        pay[p, 16:17] = jnp.zeros((1, 128), F32)
    bias = jnp.sum(g_bias[...], axis=0, keepdims=True)
    pay[0, 16:17] = stats[0:1]
    pay[1, 16:17] = stats[1:2]
    pay[2, 16:17] = bias[:, 0:128]
    pay[3, 16:17] = bias[:, 128:256]


def product_call(kernel, index, dense, out_shape, outs, scratch, name):
    return pl.pallas_call(
        kernel,
        out_shape=out_shape,
        in_specs=[SM, SM] + [VM] * (2 + len(dense)),
        out_specs=jax.tree.map(lambda _: VM, out_shape),
        scratch_shapes=scratch + [pltpu.VMEM((outs + 1, 128, 128), F32)] if name != "product_back"
        else [pltpu.VMEM((outs + 1, 128, 128), F32)] + scratch,
        compiler_params=pltpu.CompilerParams(vmem_limit_bytes=PRODUCT_LIMIT),
        name=name,
    )(*index, *dense)


class RowSum:
    def __init__(self, parts, inbox, pieces, send, recv, local):
        self.parts, self.inbox, self.send, self.recv, self.local = parts, inbox, send, recv, local
        self.rows = inbox.shape[1] // pieces
        self.r, self.c, _, _, _ = place()
        self.to, self.came = row_peers(self.r)
        self.copies, self.mine = [], []
        for s in range(pieces):
            if s and STAGGER:
                for copy in self.copies:
                    copy.wait_send()
            for i in range(7):
                self.copies.append(self.copy(i, self.r, s))
                self.copies[-1].start()
            part = pl.ds(s * self.rows, self.rows)
            self.mine.append(pltpu.make_async_copy(parts.at[self.r, part], inbox.at[self.r, part], local.at[s]))
            self.mine[-1].start()
        self.waiting = self.copies[7 * (pieces - 1):] if STAGGER else self.copies

    def copy(self, i, slot, s):
        part = pl.ds(s * self.rows, self.rows)
        return remote(self.parts.at[self.to[i], part], self.inbox.at[slot, part], self.send.at[i, s], self.recv.at[i, s], self.to[i], self.c)

    def piece(self, s):
        part = slice(s * self.rows, (s + 1) * self.rows)
        self.mine[s].wait()
        total = self.inbox[self.r, part].astype(F32)
        for i in (6, 4, 5, 1, 2, 3, 0):
            self.copy(i, self.came[i], s).wait_recv()
            total = total + self.inbox[self.came[i], part].astype(F32)
        return total

    def end(self):
        for copy in self.waiting:
            copy.wait_send()


def first_kernel(parts, strip, inbox, outgoing, send, recv, local, gsend, grecv, glocal):
    r, c, z, yl, k = place()
    to, _ = row_peers(r)
    greet([(p, c) for p in to] + [(r, n) for n in col_neighbours(z, yl, k)])
    row_sum = RowSum(parts, inbox, PIECES, send, recv, local)
    gather = Gather(outgoing, strip, PIECES, gsend, grecv, glocal)
    for n, s in ORDER:
        if n == 0:
            outgoing[gather.rows * s:gather.rows * (s + 1)] = row_sum.piece(s)
            gather.begin(s)
        else:
            gather.stage(n, s)
    gather.end()
    row_sum.end()


def first_call(parts):
    return pl.pallas_call(
        first_kernel,
        out_shape=jax.ShapeDtypeStruct((32, 256, 128), F32),
        in_specs=[ANY],
        out_specs=VM,
        scratch_shapes=[
            pltpu.VMEM((8, 256, 128), F32),
            pltpu.VMEM((256, 128), F32),
            pltpu.SemaphoreType.DMA((7, PIECES)),
            pltpu.SemaphoreType.DMA((7, PIECES)),
            pltpu.SemaphoreType.DMA((PIECES,)),
        ] + gather_scratch(PIECES),
        compiler_params=pltpu.CompilerParams(collective_id=1, has_side_effects=True, vmem_limit_bytes=LIMIT),
        name="first_layer",
    )(parts)


def second_kernel(parts, labels, train, b_second, logits, stats, grads,
                  inbox, outgoing, send, recv, local, gsend, grecv, glocal):
    r, c, z, yl, k = place()
    to, came = row_peers(r)
    greet([(p, c) for p in to])
    row_sum = RowSum(parts, inbox, 2, send, recv, local)
    classes = lax.broadcasted_iota(jnp.int32, (128, 256), 0)
    onehot = jnp.where(classes == labels[...], 1.0, 0.0).T
    mask = jnp.broadcast_to(train[...].astype(F32), (128, 256)).T
    count = 32768.0
    sends, mine = [], []
    stats[...] = jnp.zeros(stats.shape, F32)

    def grad_copy(i, slot, s):
        return remote(outgoing.at[s], grads.at[slot, s], gsend.at[i, s], grecv.at[i, s], to[i], c)

    for s in range(2):
        part = slice(128 * s, 128 * s + 128)
        scores = row_sum.piece(s) + b_second[...]
        row_max = jnp.max(scores, axis=1, keepdims=True)
        log_total = jnp.log(jnp.sum(jnp.exp(scores - row_max), axis=1, keepdims=True)) + row_max
        d_scores = mask[part] * (jnp.exp(scores - log_total) - onehot[part]) / count
        outgoing[s] = d_scores.astype(BF16)
        for i in range(7):
            sends.append(grad_copy(i, r, s))
            sends[-1].start()
        mine.append(pltpu.make_async_copy(outgoing.at[s], grads.at[r, s], glocal.at[s]))
        mine[-1].start()
        logits[part] = scores.astype(BF16)
        cross = mask[part] * onehot[part] * (log_total - scores) / count
        stats[0:1] += jnp.sum(d_scores, axis=0, keepdims=True)
        stats[1:2] += jnp.sum(cross, axis=0, keepdims=True)
    for s in range(2):
        for i in range(7):
            grad_copy(i, came[i], s).wait_recv()
        mine[s].wait()
    row_sum.end()
    for copy in sends:
        copy.wait_send()


def second_call(parts, labels, train, b_second):
    return pl.pallas_call(
        second_kernel,
        out_shape=(
            jax.ShapeDtypeStruct((256, 128), BF16),
            jax.ShapeDtypeStruct((8, 128), F32),
            jax.ShapeDtypeStruct((8, 2, 128, 128), BF16),
        ),
        in_specs=[ANY, VM, VM, VM],
        out_specs=(VM, VM, VM),
        scratch_shapes=[
            pltpu.VMEM((8, 256, 128), BF16),
            pltpu.VMEM((2, 128, 128), BF16),
        ] + 2 * [
            pltpu.SemaphoreType.DMA((7, 2)),
            pltpu.SemaphoreType.DMA((7, 2)),
            pltpu.SemaphoreType.DMA((2,)),
        ],
        compiler_params=pltpu.CompilerParams(collective_id=2, has_side_effects=True, vmem_limit_bytes=LIMIT),
        name="second_layer",
    )(parts, labels, train, b_second)


PIECE = 17


def last_kernel(pay, sums, box_t, half, box_p, box_z, t_send, t_recv, p_send, p_recv, z_send, z_recv):
    r, c, z, yl, k = place()
    me, mine16 = 4 * (r % 4) + 2 * (r // 4) + yl, 16 * k

    def on_plane(j):
        return 4 * (j % 4 // 2) + j // 4, 4 * z + 2 * (j % 2) + k

    def on_z(j):
        return r, 4 * j + 2 * yl + k

    def others(n, first, then):
        @pl.loop(1, n)
        def _(i):
            then(lax.rem(first + i, n))

    barrier = pltpu.get_barrier_semaphore()

    def signal(device):
        pl.semaphore_signal(barrier, inc=1, device_id=device, device_id_type=MESH)

    others(8, z, lambda j: signal(on_z(j)))
    others(16, me, lambda j: signal(on_plane(j)))
    twin = (r, 4 * z + 2 * yl + 1 - k)
    signal(twin)
    pl.semaphore_wait(barrier, 23)

    half_copy = remote(pay.at[pl.ds(16 - mine16, 16)], box_t, t_send.at[0], t_recv.at[0], *twin)
    half_copy.start()
    half_copy.wait_recv()
    half[...] = pay[pl.ds(mine16, 16)] + box_t[...]

    def plane_copy(j, frm):
        return remote(half.at[j], box_p.at[frm], p_send.at[0, j], p_recv.at[0, frm], *on_plane(j))

    def z_copy(j, frm):
        return remote(box_z.at[z], box_z.at[frm], z_send.at[j], z_recv.at[frm], *on_z(j))

    def plane_back(j, frm):
        block = sums.at[mine16 + frm]
        return remote(block, block, p_send.at[1, j], p_recv.at[1, frm], *on_plane(j))

    others(16, me, lambda j: plane_copy(j, me).start())
    box_p[me] = half[me]
    others(16, me, lambda j: plane_copy(j, j).wait_recv())
    total = box_p[0]
    for j in range(1, 16):
        total = total + box_p[j]
    box_z[z] = total
    others(8, z, lambda j: z_copy(j, z).start())
    others(8, z, lambda j: z_copy(j, j).wait_recv())
    total = box_z[0]
    for j in range(1, 8):
        total = total + box_z[j]
    sums[mine16 + me] = total
    others(16, me, lambda j: plane_back(j, me).start())
    others(16, me, lambda j: plane_back(j, j).wait_recv())
    back = sums.at[pl.ds(mine16, 16)]
    back_copy = remote(back, back, t_send.at[1], t_recv.at[1], *twin)
    back_copy.start()
    other_half = sums.at[pl.ds(16 - mine16, 16)]
    remote(other_half, other_half, t_send.at[1], t_recv.at[1], *twin).wait_recv()
    half_copy.wait_send()
    back_copy.wait_send()
    others(8, z, lambda j: z_copy(j, z).wait_send())
    others(16, me, lambda j: plane_copy(j, me).wait_send())
    others(16, me, lambda j: plane_back(j, me).wait_send())


def last_call(pay):
    return pl.pallas_call(
        last_kernel,
        out_shape=jax.ShapeDtypeStruct((32, PIECE, 128), F32),
        in_specs=[VM],
        out_specs=VM,
        scratch_shapes=[
            pltpu.VMEM((16, PIECE, 128), F32),
            pltpu.VMEM((16, PIECE, 128), F32),
            pltpu.VMEM((16, PIECE, 128), F32),
            pltpu.VMEM((8, PIECE, 128), F32),
            pltpu.SemaphoreType.DMA((2,)),
            pltpu.SemaphoreType.DMA((2,)),
            pltpu.SemaphoreType.DMA((2, 16)),
            pltpu.SemaphoreType.DMA((2, 16)),
            pltpu.SemaphoreType.DMA((8,)),
            pltpu.SemaphoreType.DMA((8,)),
        ],
        compiler_params=pltpu.CompilerParams(collective_id=3, has_side_effects=True, vmem_limit_bytes=LIMIT),
        name="weight_gradients",
    )(pay)


def finish_kernel(sums, scores, logits, loss, g_first, b_first, g_second, b_second):
    logits[...] = scores[...]
    for p in range(8):
        g_first[16 * p:16 * p + 16, 0:128] = sums[p, 0:16]
        g_first[16 * p:16 * p + 16, 128:256] = sums[p + 8, 0:16]
    for p in range(16):
        g_second[16 * p:16 * p + 16] = sums[p + 16, 0:16]
    b_second[...] = sums[0, 16:17]
    loss[...] = jnp.sum(sums[1, 16:17], axis=1, keepdims=True)
    b_first[:, 0:128] = sums[2, 16:17]
    b_first[:, 128:256] = sums[3, 16:17]


def finish_call(sums, scores):
    return pl.pallas_call(
        finish_kernel,
        out_shape=(
            jax.ShapeDtypeStruct((256, 128), BF16),
            jax.ShapeDtypeStruct((1, 1), F32),
            jax.ShapeDtypeStruct((128, 256), F32),
            jax.ShapeDtypeStruct((1, 256), F32),
            jax.ShapeDtypeStruct((256, 128), F32),
            jax.ShapeDtypeStruct((1, 128), F32),
        ),
        in_specs=[VM, VM],
        out_specs=(VM,) * 6,
        compiler_params=pltpu.CompilerParams(vmem_limit_bytes=4 * 1024 * 1024),
        name="outputs",
    )(sums, scores)


def local(features, labels, train_mask, adj_rows, adj_cols, adj_live, adj_values, w_first, b_first, w_second, b_second):
    strip, blocks = gather_call(features, adj_values[0, 0])
    index = (adj_rows, adj_cols, adj_live, blocks)
    shape = jax.ShapeDtypeStruct
    part = product_call(
        product_first_kernel, index, (strip.reshape(64, 128, 128),), shape((16, 128, 128), F32), 16, [], "product_first"
    )
    agg = first_call(part.reshape(8, 256, 128)).reshape(64, 128, 128)
    part, hidden = product_call(
        product_second_kernel, index, (agg, w_first, b_first.reshape(1, 256), w_second),
        (shape((16, 128, 128), BF16), shape((64, 128, 256), BF16)), 16, [pltpu.VMEM((64, 128, 128), BF16)], "product_second",
    )
    scores, stats, grads = second_call(
        part.reshape(8, 256, 128), labels.reshape(1, 256), train_mask.reshape(1, 256), b_second.reshape(1, 128)
    )
    pay = product_call(
        product_back_kernel, index, (grads.reshape(16, 128, 128), agg, hidden, w_second, stats),
        shape((32, PIECE, 128), F32), 64,
        [pltpu.VMEM((128, 256), F32), pltpu.VMEM((256, 128), F32), pltpu.VMEM((8, 256), F32)], "product_back",
    )
    sums = last_call(pay)
    logits, loss, g_first, gb_first, g_second, gb_second = finish_call(sums, scores)
    return logits, loss.reshape(()), g_first, gb_first.reshape(256), g_second, gb_second.reshape(128)


def solution(mesh):
    in_specs = (
        P(("row", "col"), None),
        P(("row", "col")),
        P(("row", "col")),
        P("row", "col", None),
        P("row", "col", None),
        P("row", "col"),
        P("row", "col", None, None, None),
        P(),
        P(),
        P(),
        P(),
    )
    out_specs = (P(("row", "col"), None), P(), P(), P(), P(), P())
    return jax.shard_map(local, mesh=mesh, in_specs=in_specs, out_specs=out_specs, check_vma=False)
```

```python
import functools

import jax
import jax.numpy as jnp
from jax import lax
from jax.experimental import pallas as pl
from jax.experimental.pallas import tpu as pltpu
from jax.sharding import PartitionSpec as P

MESH = pl.DeviceIdType.MESH
F32, BF16 = jnp.float32, jnp.bfloat16
ANY = pl.BlockSpec(memory_space=pl.ANY)
VM = pl.BlockSpec(memory_space=pltpu.VMEM)
SM = pl.BlockSpec(memory_space=pltpu.SMEM)
LIMIT = 32 * 1024 * 1024
PRODUCT_LIMIT = 24 * 1024 * 1024
UNROLL = 32
STEP = 2048
PIECES, STAGGER = 2, False
LOADS = 4


def dot(a, b):
    return jnp.dot(a, b, preferred_element_type=F32)


def dot_tn(a, b):
    return lax.dot_general(a, b, (((0,), (0,)), ((), ())), preferred_element_type=F32)


def halves(a):
    hi = a.astype(BF16)
    return hi, (a - hi.astype(F32)).astype(BF16)


def place():
    r, c = lax.axis_index("row"), lax.axis_index("col")
    return r, c, c // 4, (c // 2) % 2, c % 2


def remote(src, dst, send, recv, r, c):
    return pltpu.make_async_remote_copy(
        src_ref=src, dst_ref=dst, send_sem=send, recv_sem=recv,
        device_id=(r, c), device_id_type=MESH,
    )


def col_neighbours(z, yl, k):
    up, down = (z + 1) % 8, (z + 7) % 8
    return (4 * up + 2 * yl + k, 4 * down + 2 * yl + k, 4 * z + 2 * (1 - yl) + k, 4 * z + 2 * yl + 1 - k)


def row_peers(r):
    x, yh = r % 4, r // 4
    to, came = [], []
    for dy, dx in ((1, 2), (0, 2), (1, 1), (1, 3), (0, 1), (0, 3), (1, 0)):
        y2 = (yh + dy) % 2
        to.append(4 * y2 + (x + dx) % 4)
        came.append(4 * y2 + (x + 4 - dx) % 4)
    return to, came


def greet(devices):
    barrier = pltpu.get_barrier_semaphore()
    for device in devices:
        pl.semaphore_signal(barrier, inc=1, device_id=device, device_id_type=MESH)
    pl.semaphore_wait(barrier, len(devices))


def gather_scratch(pieces):
    return [
        pltpu.SemaphoreType.DMA((36 * pieces,)),
        pltpu.SemaphoreType.DMA((32, pieces)),
        pltpu.SemaphoreType.DMA((pieces,)),
    ]


class Gather:
    STAGES = (
        ((-1, False, "ut"), (1, False, "dt"), (0, True, "udt")),
        ((-2, False, "uat"), (2, False, "dt"), (1, True, "dt"), (-1, True, "t")),
        ((-3, False, "uat"), (3, False, "at"), (2, True, "t"), (-2, True, "t")),
        ((-4, False, "at"), (-3, True, "t"), (3, True, "t")),
        ((-4, True, "t"),),
    )

    def __init__(self, src, out, pieces, send, recv, local):
        self.src, self.out, self.pieces, self.send, self.recv, self.local = src, out, pieces, send, recv, local
        self.rows = src.shape[0] // pieces
        self.r, self.c, self.z, self.yl, self.k = place()
        up, down, across, twin = col_neighbours(self.z, self.yl, self.k)
        self.to = {"u": up, "d": down, "a": across, "t": twin}
        self.started, self.kept = [], []

    def slot(self, dz, other):
        return 4 * ((self.z + dz + 8) % 8) + 2 * (1 - self.yl if other else self.yl) + self.k

    def part(self, slot, s):
        return self.out.at[slot, pl.ds(s * self.rows, self.rows)]

    def push(self, block, slot, s, targets):
        for name in targets:
            copy = remote(block, self.part(slot, s), self.send.at[len(self.started)], self.recv.at[slot, s], self.r, self.to[name])
            copy.start()
            self.started.append(copy)

    def arrived(self, slot, s):
        block = self.part(slot, s)
        remote(block, block, self.send.at[0], self.recv.at[slot, s], self.r, self.to["t"]).wait_recv()

    def begin(self, s):
        block = self.src.at[pl.ds(s * self.rows, self.rows)]
        self.push(block, self.c, s, "udat")
        mine = pltpu.make_async_copy(block, self.part(self.c, s), self.local.at[s])
        mine.start()
        self.kept.append(mine)

    def stage(self, n, s):
        for dz, other, targets in self.STAGES[n - 1]:
            slot = self.slot(dz, other)
            self.arrived(slot, s)
            self.push(self.part(slot, s), slot, s, targets)

    def end(self):
        for s in range(self.pieces):
            for dz in range(8):
                for other in (False, True):
                    self.arrived(self.slot(dz, other) + 1 - 2 * self.k, s)
        for copy in self.kept:
            copy.wait()
        for copy in self.started:
            copy.wait_send()


def gather_kernel(src, blocks, out, held, load_sem, *sems):
    r, c, z, yl, k = place()
    greet([(r, n) for n in col_neighbours(z, yl, k)])
    gather = Gather(src, out, 1, *sems)
    gather.begin(0)
    share = blocks.shape[0] // LOADS
    loads = [
        pltpu.make_async_copy(blocks.at[pl.ds(i * share, share)], held.at[pl.ds(i * share, share)], load_sem.at[i])
        for i in range(LOADS)
    ]
    for load in loads:
        load.start()
    for n in range(1, 6):
        gather.stage(n, 0)
    gather.end()
    for load in loads:
        load.wait()


def gather_call(features, blocks):
    return pl.pallas_call(
        gather_kernel,
        out_shape=(
            jax.ShapeDtypeStruct((32,) + features.shape, BF16),
            jax.ShapeDtypeStruct(blocks.shape, BF16),
        ),
        in_specs=[ANY, ANY],
        out_specs=(VM, VM),
        scratch_shapes=[pltpu.SemaphoreType.DMA((LOADS,))] + gather_scratch(1),
        compiler_params=pltpu.CompilerParams(collective_id=0, has_side_effects=True, vmem_limit_bytes=LIMIT),
        name="gather_features",
    )(pltpu.with_memory_space_constraint(features, pltpu.HBM), pltpu.with_memory_space_constraint(blocks, pltpu.HBM))


def sparse_product(backward, rows, cols, live, blocks, source, total):
    n = jnp.max(live[...])
    outs = total.shape[0] - 1

    @pl.loop(0, outs, unroll=2)
    def _(i):
        total[i] = jnp.zeros(total.shape[1:], F32)

    @pl.loop(0, (n + UNROLL - 1) // UNROLL)
    def _(u):
        products, targets = [], []
        for i in range(UNROLL):
            b = u * UNROLL + i
            row, col = rows[0, 0, b], cols[0, 0, b]
            if backward:
                products.append(dot_tn(blocks[b], source[row]))
                targets.append(jnp.where(b < n, col, outs))
            else:
                products.append(dot(blocks[b], source[col]))
                targets.append(jnp.where(b < n, row, outs))
        for product, target in zip(products, targets):
            total[target] += product


def product_first_kernel(rows, cols, live, blocks, source, out, total):
    sparse_product(False, rows, cols, live, blocks, source, total)

    @pl.loop(0, out.shape[0], unroll=2)
    def _(i):
        out[i] = total[i]


def product_second_kernel(rows, cols, live, blocks, source, out, total):
    sparse_product(False, rows, cols, live, blocks, source, total)

    @pl.loop(0, out.shape[0], unroll=2)
    def _(i):
        out[i] = total[i].astype(BF16)


def product_back_kernel(rows, cols, live, blocks, source, total):
    sparse_product(True, rows, cols, live, blocks, source, total)


def product_call(kernel, index, dense, out_shape, scratch, name):
    return pl.pallas_call(
        kernel,
        out_shape=out_shape,
        in_specs=[SM, SM] + [VM] * (2 + len(dense)),
        out_specs=jax.tree.map(lambda _: VM, out_shape),
        scratch_shapes=scratch,
        compiler_params=pltpu.CompilerParams(vmem_limit_bytes=PRODUCT_LIMIT),
        name=name,
    )(*index, *dense)


class RowSum:
    def __init__(self, parts, inbox, pieces, send, recv, local):
        self.parts, self.inbox, self.send, self.recv, self.local = parts, inbox, send, recv, local
        self.rows = inbox.shape[1] // pieces
        self.r, self.c, _, _, _ = place()
        self.to, self.came = row_peers(self.r)
        self.copies, self.mine = [], []
        for s in range(pieces):
            if s and STAGGER:
                for copy in self.copies:
                    copy.wait_send()
            for i in range(7):
                self.copies.append(self.copy(i, self.r, s))
                self.copies[-1].start()
            part = pl.ds(s * self.rows, self.rows)
            self.mine.append(pltpu.make_async_copy(parts.at[self.r, part], inbox.at[self.r, part], local.at[s]))
            self.mine[-1].start()
        self.waiting = self.copies[7 * (pieces - 1):] if STAGGER else self.copies

    def copy(self, i, slot, s):
        part = pl.ds(s * self.rows, self.rows)
        return remote(self.parts.at[self.to[i], part], self.inbox.at[slot, part], self.send.at[i, s], self.recv.at[i, s], self.to[i], self.c)

    def piece(self, s):
        part = slice(s * self.rows, (s + 1) * self.rows)
        self.mine[s].wait()
        total = self.inbox[self.r, part].astype(F32)
        for i in (6, 4, 5, 1, 2, 3, 0):
            self.copy(i, self.came[i], s).wait_recv()
            total = total + self.inbox[self.came[i], part].astype(F32)
        return total

    def end(self):
        for copy in self.waiting:
            copy.wait_send()


def first_kernel(parts, w_first, b_first, w_second, strip, hidden, scaled,
                 inbox, outgoing, send, recv, local, gsend, grecv, glocal):
    r, c, z, yl, k = place()
    to, _ = row_peers(r)
    greet([(p, c) for p in to] + [(r, n) for n in col_neighbours(z, yl, k)])
    row_sum = RowSum(parts, inbox, PIECES, send, recv, local)
    gather = Gather(outgoing, strip, PIECES, gsend, grecv, glocal)

    def dense(slots):
        kept = []
        for slot in slots:
            high, low = halves(strip[slot])
            pre = dot(high, w_first[...]) + dot(low, w_first[...]) + b_first[...]
            kept.append(jnp.maximum(pre, 0.0).astype(BF16))
        products = [dot(one, w_second[...]).astype(BF16) for one in kept]
        for slot, one, product in zip(slots, kept, products):
            hidden[slot] = one
            scaled[slot] = product

    def of_stage(n):
        return [gather.slot(dz, other) for dz, other, _ in (gather.STAGES[n - 1] if n else ((0, False, ""),))]

    def of_twin(n):
        slots = [slot + 1 - 2 * k for slot in of_stage(n)]
        for slot in slots:
            for s in range(PIECES):
                gather.arrived(slot, s)
        return slots

    for s in range(PIECES):
        outgoing[gather.rows * s:gather.rows * (s + 1)] = row_sum.piece(s)
        gather.begin(s)
    for copy in gather.kept:
        copy.wait()
    dense(of_stage(0))
    for n in range(1, 6):
        for s in range(PIECES):
            gather.stage(n, s)
        dense(of_stage(n) + (of_twin(n - 1) if n < 5 else []))
        if n == 4:
            dense(of_twin(4))
    dense(of_twin(5))
    for copy in gather.started:
        copy.wait_send()
    row_sum.end()


def first_call(parts, w_first, b_first, w_second):
    return pl.pallas_call(
        first_kernel,
        out_shape=(
            jax.ShapeDtypeStruct((32, 256, 128), F32),
            jax.ShapeDtypeStruct((32, 256, 256), BF16),
            jax.ShapeDtypeStruct((32, 256, 128), BF16),
        ),
        in_specs=[ANY, VM, VM, VM],
        out_specs=(VM, VM, VM),
        scratch_shapes=[
            pltpu.VMEM((8, 256, 128), F32),
            pltpu.VMEM((256, 128), F32),
            pltpu.SemaphoreType.DMA((7, PIECES)),
            pltpu.SemaphoreType.DMA((7, PIECES)),
            pltpu.SemaphoreType.DMA((PIECES,)),
        ] + gather_scratch(PIECES),
        compiler_params=pltpu.CompilerParams(collective_id=1, has_side_effects=True, vmem_limit_bytes=LIMIT),
        name="first_layer",
    )(parts, w_first, b_first, w_second)


def second_kernel(parts, labels, train, b_second, logits, stats, grads,
                  inbox, outgoing, send, recv, local, gsend, grecv, glocal):
    r, c, z, yl, k = place()
    to, came = row_peers(r)
    greet([(p, c) for p in to])
    row_sum = RowSum(parts, inbox, 2, send, recv, local)
    classes = lax.broadcasted_iota(jnp.int32, (128, 256), 0)
    onehot = jnp.where(classes == labels[...], 1.0, 0.0).T
    mask = jnp.broadcast_to(train[...].astype(F32), (128, 256)).T
    count = 32768.0
    sends, mine = [], []
    stats[...] = jnp.zeros(stats.shape, F32)

    def grad_copy(i, slot, s):
        return remote(outgoing.at[s], grads.at[slot, s], gsend.at[i, s], grecv.at[i, s], to[i], c)

    for s in range(2):
        part = slice(128 * s, 128 * s + 128)
        scores = row_sum.piece(s) + b_second[...]
        row_max = jnp.max(scores, axis=1, keepdims=True)
        log_total = jnp.log(jnp.sum(jnp.exp(scores - row_max), axis=1, keepdims=True)) + row_max
        d_scores = mask[part] * (jnp.exp(scores - log_total) - onehot[part]) / count
        outgoing[s] = d_scores.astype(BF16)
        for i in range(7):
            sends.append(grad_copy(i, r, s))
            sends[-1].start()
        mine.append(pltpu.make_async_copy(outgoing.at[s], grads.at[r, s], glocal.at[s]))
        mine[-1].start()
        logits[part] = scores.astype(BF16)
        cross = mask[part] * onehot[part] * (log_total - scores) / count
        stats[0:1] += jnp.sum(d_scores, axis=0, keepdims=True)
        stats[1:2] += jnp.sum(cross, axis=0, keepdims=True)
    for s in range(2):
        for i in range(7):
            grad_copy(i, came[i], s).wait_recv()
        mine[s].wait()
    row_sum.end()
    for copy in sends:
        copy.wait_send()


def second_call(parts, labels, train, b_second):
    return pl.pallas_call(
        second_kernel,
        out_shape=(
            jax.ShapeDtypeStruct((256, 128), BF16),
            jax.ShapeDtypeStruct((8, 128), F32),
            jax.ShapeDtypeStruct((8, 2, 128, 128), BF16),
        ),
        in_specs=[ANY, VM, VM, VM],
        out_specs=(VM, VM, VM),
        scratch_shapes=[
            pltpu.VMEM((8, 256, 128), BF16),
            pltpu.VMEM((2, 128, 128), BF16),
        ] + 2 * [
            pltpu.SemaphoreType.DMA((7, 2)),
            pltpu.SemaphoreType.DMA((7, 2)),
            pltpu.SemaphoreType.DMA((2,)),
        ],
        compiler_params=pltpu.CompilerParams(collective_id=2, has_side_effects=True, vmem_limit_bytes=LIMIT),
        name="second_layer",
    )(parts, labels, train, b_second)


PIECE = 17


def weight_gradients(total, agg, hidden, w_second, stats, pay, g_first, g_second, g_bias):
    nodes = STEP // 128
    w_second_t = w_second[...].astype(F32).T.astype(BF16)
    g_first[...] = jnp.zeros(g_first.shape, F32)
    g_second[...] = jnp.zeros(g_second.shape, F32)
    g_bias[...] = jnp.zeros(g_bias.shape, F32)

    @pl.loop(0, hidden.shape[0] // nodes)
    def _(i):
        part = pl.ds(i * nodes, nodes)
        grad = total[part].reshape(STEP, 128).astype(BF16)
        kept = hidden[part].reshape(STEP, 256)
        d_pre = jnp.where(kept > 0, dot(grad, w_second_t), 0.0)
        g_second[...] += dot_tn(kept, grad)
        g_first[...] += dot_tn(agg[part].reshape(STEP, 128).astype(BF16), d_pre.astype(BF16))
        g_bias[...] += jnp.sum(d_pre.reshape(STEP // 8, 8, 256), axis=0)

    for p in range(8):
        pay[p, 0:16] = g_first[16 * p:16 * p + 16, 0:128]
        pay[p + 8, 0:16] = g_first[16 * p:16 * p + 16, 128:256]
    for p in range(16):
        pay[p + 16, 0:16] = g_second[16 * p:16 * p + 16]
    for p in range(4, 32):
        pay[p, 16:17] = jnp.zeros((1, 128), F32)
    bias = jnp.sum(g_bias[...], axis=0, keepdims=True)
    pay[0, 16:17] = stats[0:1]
    pay[1, 16:17] = stats[1:2]
    pay[2, 16:17] = bias[:, 0:128]
    pay[3, 16:17] = bias[:, 128:256]


def last_kernel(total_back, agg, hidden, w_second, stats, sums, pay, g_first, g_second, g_bias, box_t, half, box_p, box_z, t_send, t_recv, p_send, p_recv, z_send, z_recv):
    r, c, z, yl, k = place()
    me, mine16 = 4 * (r % 4) + 2 * (r // 4) + yl, 16 * k

    def on_plane(j):
        return 4 * (j % 4 // 2) + j // 4, 4 * z + 2 * (j % 2) + k

    def on_z(j):
        return r, 4 * j + 2 * yl + k

    def others(n, first, then):
        @pl.loop(1, n)
        def _(i):
            then(lax.rem(first + i, n))

    barrier = pltpu.get_barrier_semaphore()

    def signal(device):
        pl.semaphore_signal(barrier, inc=1, device_id=device, device_id_type=MESH)

    others(8, z, lambda j: signal(on_z(j)))
    others(16, me, lambda j: signal(on_plane(j)))
    twin = (r, 4 * z + 2 * yl + 1 - k)
    signal(twin)
    weight_gradients(total_back, agg, hidden, w_second, stats, pay, g_first, g_second, g_bias)
    pl.semaphore_wait(barrier, 23)

    half_copy = remote(pay.at[pl.ds(16 - mine16, 16)], box_t, t_send.at[0], t_recv.at[0], *twin)
    half_copy.start()
    half_copy.wait_recv()
    half[...] = pay[pl.ds(mine16, 16)] + box_t[...]

    def plane_copy(j, frm):
        return remote(half.at[j], box_p.at[frm], p_send.at[0, j], p_recv.at[0, frm], *on_plane(j))

    def z_copy(j, frm):
        return remote(box_z.at[z], box_z.at[frm], z_send.at[j], z_recv.at[frm], *on_z(j))

    def plane_back(j, frm):
        block = sums.at[mine16 + frm]
        return remote(block, block, p_send.at[1, j], p_recv.at[1, frm], *on_plane(j))

    others(16, me, lambda j: plane_copy(j, me).start())
    box_p[me] = half[me]
    others(16, me, lambda j: plane_copy(j, j).wait_recv())
    total = box_p[0]
    for j in range(1, 16):
        total = total + box_p[j]
    box_z[z] = total
    others(8, z, lambda j: z_copy(j, z).start())
    others(8, z, lambda j: z_copy(j, j).wait_recv())
    total = box_z[0]
    for j in range(1, 8):
        total = total + box_z[j]
    sums[mine16 + me] = total
    others(16, me, lambda j: plane_back(j, me).start())
    others(16, me, lambda j: plane_back(j, j).wait_recv())
    back = sums.at[pl.ds(mine16, 16)]
    back_copy = remote(back, back, t_send.at[1], t_recv.at[1], *twin)
    back_copy.start()
    other_half = sums.at[pl.ds(16 - mine16, 16)]
    remote(other_half, other_half, t_send.at[1], t_recv.at[1], *twin).wait_recv()
    half_copy.wait_send()
    back_copy.wait_send()
    others(8, z, lambda j: z_copy(j, z).wait_send())
    others(16, me, lambda j: plane_copy(j, me).wait_send())
    others(16, me, lambda j: plane_back(j, me).wait_send())


def last_call(*dense):
    return pl.pallas_call(
        last_kernel,
        out_shape=jax.ShapeDtypeStruct((32, PIECE, 128), F32),
        in_specs=[VM] * 5,
        out_specs=VM,
        scratch_shapes=[
            pltpu.VMEM((32, PIECE, 128), F32),
            pltpu.VMEM((128, 256), F32),
            pltpu.VMEM((256, 128), F32),
            pltpu.VMEM((8, 256), F32),
            pltpu.VMEM((16, PIECE, 128), F32),
            pltpu.VMEM((16, PIECE, 128), F32),
            pltpu.VMEM((16, PIECE, 128), F32),
            pltpu.VMEM((8, PIECE, 128), F32),
            pltpu.SemaphoreType.DMA((2,)),
            pltpu.SemaphoreType.DMA((2,)),
            pltpu.SemaphoreType.DMA((2, 16)),
            pltpu.SemaphoreType.DMA((2, 16)),
            pltpu.SemaphoreType.DMA((8,)),
            pltpu.SemaphoreType.DMA((8,)),
        ],
        compiler_params=pltpu.CompilerParams(collective_id=3, has_side_effects=True, vmem_limit_bytes=LIMIT),
        name="weight_gradients",
    )(*dense)


def finish_kernel(sums, scores, logits, loss, g_first, b_first, g_second, b_second):
    logits[...] = scores[...]
    for p in range(8):
        g_first[16 * p:16 * p + 16, 0:128] = sums[p, 0:16]
        g_first[16 * p:16 * p + 16, 128:256] = sums[p + 8, 0:16]
    for p in range(16):
        g_second[16 * p:16 * p + 16] = sums[p + 16, 0:16]
    b_second[...] = sums[0, 16:17]
    loss[...] = jnp.sum(sums[1, 16:17], axis=1, keepdims=True)
    b_first[:, 0:128] = sums[2, 16:17]
    b_first[:, 128:256] = sums[3, 16:17]


def finish_call(sums, scores):
    return pl.pallas_call(
        finish_kernel,
        out_shape=(
            jax.ShapeDtypeStruct((256, 128), BF16),
            jax.ShapeDtypeStruct((1, 1), F32),
            jax.ShapeDtypeStruct((128, 256), F32),
            jax.ShapeDtypeStruct((1, 256), F32),
            jax.ShapeDtypeStruct((256, 128), F32),
            jax.ShapeDtypeStruct((1, 128), F32),
        ),
        in_specs=[VM, VM],
        out_specs=(VM,) * 6,
        compiler_params=pltpu.CompilerParams(vmem_limit_bytes=4 * 1024 * 1024),
        name="outputs",
    )(sums, scores)


def local(features, labels, train_mask, adj_rows, adj_cols, adj_live, adj_values, w_first, b_first, w_second, b_second):
    strip, blocks = gather_call(features, adj_values[0, 0])
    index = (adj_rows, adj_cols, adj_live, blocks)
    shape = jax.ShapeDtypeStruct
    part = product_call(
        product_first_kernel, index, (strip.reshape(64, 128, 128),), shape((16, 128, 128), F32), [pltpu.VMEM((17, 128, 128), F32)],
        "product_first",
    )
    agg, hidden, scaled = first_call(part.reshape(8, 256, 128), w_first, b_first.reshape(1, 256), w_second)
    part = product_call(
        product_second_kernel, index, (scaled.reshape(64, 128, 128),), shape((16, 128, 128), BF16),
        [pltpu.VMEM((17, 128, 128), F32)], "product_second",
    )
    scores, stats, grads = second_call(
        part.reshape(8, 256, 128), labels.reshape(1, 256), train_mask.reshape(1, 256), b_second.reshape(1, 128)
    )
    total = product_call(
        product_back_kernel, index, (grads.reshape(16, 128, 128),), shape((65, 128, 128), F32), [], "product_back"
    )
    sums = last_call(total, agg.reshape(64, 128, 128), hidden.reshape(64, 128, 256), w_second, stats)
    logits, loss, g_first, gb_first, g_second, gb_second = finish_call(sums, scores)
    return logits, loss.reshape(()), g_first, gb_first.reshape(256), g_second, gb_second.reshape(128)


def solution(mesh):
    in_specs = (
        P(("row", "col"), None),
        P(("row", "col")),
        P(("row", "col")),
        P("row", "col", None),
        P("row", "col", None),
        P("row", "col"),
        P("row", "col", None, None, None),
        P(),
        P(),
        P(),
        P(),
    )
    out_specs = (P(("row", "col"), None), P(), P(), P(), P(), P())
    return jax.shard_map(local, mesh=mesh, in_specs=in_specs, out_specs=out_specs, check_vma=False)
```

```python
import functools

import jax
import jax.numpy as jnp
from jax import lax
from jax.experimental import pallas as pl
from jax.experimental.pallas import tpu as pltpu
from jax.sharding import PartitionSpec as P

MESH = pl.DeviceIdType.MESH
F32, BF16 = jnp.float32, jnp.bfloat16
ANY = pl.BlockSpec(memory_space=pl.ANY)
VM = pl.BlockSpec(memory_space=pltpu.VMEM)
SM = pl.BlockSpec(memory_space=pltpu.SMEM)
LIMIT = 32 * 1024 * 1024
PRODUCT_LIMIT = 24 * 1024 * 1024
UNROLL = 32
STEP = 4096
PIECES, STAGGER = 2, False
LOADS = 4


def dot(a, b):
    return jnp.dot(a, b, preferred_element_type=F32)


def dot_tn(a, b):
    return lax.dot_general(a, b, (((0,), (0,)), ((), ())), preferred_element_type=F32)


def halves(a):
    hi = a.astype(BF16)
    return hi, (a - hi.astype(F32)).astype(BF16)


def place():
    r, c = lax.axis_index("row"), lax.axis_index("col")
    return r, c, c // 4, (c // 2) % 2, c % 2


def remote(src, dst, send, recv, r, c):
    return pltpu.make_async_remote_copy(
        src_ref=src, dst_ref=dst, send_sem=send, recv_sem=recv,
        device_id=(r, c), device_id_type=MESH,
    )


def col_neighbours(z, yl, k):
    up, down = (z + 1) % 8, (z + 7) % 8
    return (4 * up + 2 * yl + k, 4 * down + 2 * yl + k, 4 * z + 2 * (1 - yl) + k, 4 * z + 2 * yl + 1 - k)


def second_neighbours(z, yl, k):
    return 4 * ((z + 2) % 8) + 2 * yl + k, 4 * ((z + 6) % 8) + 2 * yl + k


def row_peers(r):
    x, yh = r % 4, r // 4
    to, came = [], []
    for dy, dx in ((1, 2), (0, 2), (1, 1), (1, 3), (0, 1), (0, 3), (1, 0)):
        y2 = (yh + dy) % 2
        to.append(4 * y2 + (x + dx) % 4)
        came.append(4 * y2 + (x + 4 - dx) % 4)
    return to, came


def greet(devices):
    barrier = pltpu.get_barrier_semaphore()
    for device in devices:
        pl.semaphore_signal(barrier, inc=1, device_id=device, device_id_type=MESH)
    pl.semaphore_wait(barrier, len(devices))


def gather_scratch(pieces):
    return [
        pltpu.SemaphoreType.DMA((36 * pieces,)),
        pltpu.SemaphoreType.DMA((32, pieces)),
        pltpu.SemaphoreType.DMA((pieces,)),
    ]


class Gather:
    STAGES = (
        ((-1, False, "ut"), (1, False, "dt"), (0, True, "udt")),
        ((-2, False, "uat"), (2, False, "dt"), (1, True, "dt"), (-1, True, "t")),
        ((-3, False, "uat"), (3, False, "at"), (2, True, "t"), (-2, True, "t")),
        ((-4, False, "at"), (-3, True, "t"), (3, True, "t")),
        ((-4, True, "t"),),
    )

    DIRECT = (
        ((-1, False, "at"), (1, False, "at"), (0, True, "t")),
        ((-2, False, "uUat"), (2, False, "dat")),
        ((-1, True, "t"), (1, True, "t"), (-2, True, "t"), (2, True, "t")),
        ((-3, False, "at"), (3, False, "at")),
        ((-4, False, "at"),),
        ((-3, True, "t"), (3, True, "t"), (-4, True, "t")),
    )

    def __init__(self, src, out, pieces, send, recv, local):
        self.src, self.out, self.pieces, self.send, self.recv, self.local = src, out, pieces, send, recv, local
        self.rows = src.shape[0] // pieces
        self.r, self.c, self.z, self.yl, self.k = place()
        up, down, across, twin = col_neighbours(self.z, self.yl, self.k)
        up2, down2 = second_neighbours(self.z, self.yl, self.k)
        self.to = {"u": up, "d": down, "a": across, "t": twin, "U": up2, "D": down2}
        self.started, self.kept = [], []

    def slot(self, dz, other):
        return 4 * ((self.z + dz + 8) % 8) + 2 * (1 - self.yl if other else self.yl) + self.k

    def part(self, slot, s):
        return self.out.at[slot, pl.ds(s * self.rows, self.rows)]

    def push(self, block, slot, s, targets):
        for name in targets:
            copy = remote(block, self.part(slot, s), self.send.at[len(self.started)], self.recv.at[slot, s], self.r, self.to[name])
            copy.start()
            self.started.append(copy)

    def arrived(self, slot, s):
        block = self.part(slot, s)
        remote(block, block, self.send.at[0], self.recv.at[slot, s], self.r, self.to["t"]).wait_recv()

    def begin(self, s, targets="udat"):
        block = self.src.at[pl.ds(s * self.rows, self.rows)]
        self.push(block, self.c, s, targets)
        mine = pltpu.make_async_copy(block, self.part(self.c, s), self.local.at[s])
        mine.start()
        self.kept.append(mine)

    def stage(self, n, s, stages=STAGES):
        for dz, other, targets in stages[n - 1]:
            slot = self.slot(dz, other)
            self.arrived(slot, s)
            self.push(self.part(slot, s), slot, s, targets)

    def end(self):
        for s in range(self.pieces):
            for dz in range(8):
                for other in (False, True):
                    self.arrived(self.slot(dz, other) + 1 - 2 * self.k, s)
        for copy in self.kept:
            copy.wait()
        for copy in self.started:
            copy.wait_send()


def gather_kernel(src, blocks, out, held, load_sem, *sems):
    r, c, z, yl, k = place()
    greet([(r, n) for n in col_neighbours(z, yl, k) + second_neighbours(z, yl, k)])
    gather = Gather(src, out, 1, *sems)
    gather.begin(0, "audUDt")
    share = blocks.shape[0] // LOADS
    loads = [
        pltpu.make_async_copy(blocks.at[pl.ds(i * share, share)], held.at[pl.ds(i * share, share)], load_sem.at[i])
        for i in range(LOADS)
    ]
    for load in loads:
        load.start()
    for n in range(1, 7):
        gather.stage(n, 0, gather.DIRECT)
    gather.end()
    for load in loads:
        load.wait()


def gather_call(features, blocks):
    return pl.pallas_call(
        gather_kernel,
        out_shape=(
            jax.ShapeDtypeStruct((32,) + features.shape, BF16),
            jax.ShapeDtypeStruct(blocks.shape, BF16),
        ),
        in_specs=[ANY, ANY],
        out_specs=(VM, VM),
        scratch_shapes=[pltpu.SemaphoreType.DMA((LOADS,))] + gather_scratch(1),
        compiler_params=pltpu.CompilerParams(collective_id=0, has_side_effects=True, vmem_limit_bytes=LIMIT),
        name="gather_features",
    )(pltpu.with_memory_space_constraint(features, pltpu.HBM), pltpu.with_memory_space_constraint(blocks, pltpu.HBM))


def sparse_product(backward, rows, cols, live, blocks, source, total):
    n = jnp.max(live[...])
    outs = total.shape[0] - 1

    @pl.loop(0, outs, unroll=2)
    def _(i):
        total[i] = jnp.zeros(total.shape[1:], F32)

    @pl.loop(0, (n + UNROLL - 1) // UNROLL)
    def _(u):
        products, targets = [], []
        for i in range(UNROLL):
            b = u * UNROLL + i
            row, col = rows[0, 0, b], cols[0, 0, b]
            if backward:
                products.append(dot_tn(blocks[b], source[row]))
                targets.append(jnp.where(b < n, col, outs))
            else:
                products.append(dot(blocks[b], source[col]))
                targets.append(jnp.where(b < n, row, outs))
        for product, target in zip(products, targets):
            total[target] += product


def product_first_kernel(rows, cols, live, blocks, source, out, total):
    sparse_product(False, rows, cols, live, blocks, source, total)

    @pl.loop(0, out.shape[0], unroll=2)
    def _(i):
        out[i] = total[i]


def product_second_kernel(rows, cols, live, blocks, source, out, total):
    sparse_product(False, rows, cols, live, blocks, source, total)

    @pl.loop(0, out.shape[0], unroll=2)
    def _(i):
        out[i] = total[i].astype(BF16)


def product_back_kernel(rows, cols, live, blocks, source, total):
    sparse_product(True, rows, cols, live, blocks, source, total)


def product_call(kernel, index, dense, out_shape, scratch, name):
    return pl.pallas_call(
        kernel,
        out_shape=out_shape,
        in_specs=[SM, SM] + [VM] * (2 + len(dense)),
        out_specs=jax.tree.map(lambda _: VM, out_shape),
        scratch_shapes=scratch,
        compiler_params=pltpu.CompilerParams(vmem_limit_bytes=PRODUCT_LIMIT),
        name=name,
    )(*index, *dense)


class RowSum:
    def __init__(self, parts, inbox, pieces, send, recv, local):
        self.parts, self.inbox, self.send, self.recv, self.local = parts, inbox, send, recv, local
        self.rows = inbox.shape[1] // pieces
        self.r, self.c, _, _, _ = place()
        self.to, self.came = row_peers(self.r)
        self.copies, self.mine = [], []
        for s in range(pieces):
            if s and STAGGER:
                for copy in self.copies:
                    copy.wait_send()
            for i in range(7):
                self.copies.append(self.copy(i, self.r, s))
                self.copies[-1].start()
            part = pl.ds(s * self.rows, self.rows)
            self.mine.append(pltpu.make_async_copy(parts.at[self.r, part], inbox.at[self.r, part], local.at[s]))
            self.mine[-1].start()
        self.waiting = self.copies[7 * (pieces - 1):] if STAGGER else self.copies

    def copy(self, i, slot, s):
        part = pl.ds(s * self.rows, self.rows)
        return remote(self.parts.at[self.to[i], part], self.inbox.at[slot, part], self.send.at[i, s], self.recv.at[i, s], self.to[i], self.c)

    def piece(self, s):
        part = slice(s * self.rows, (s + 1) * self.rows)
        self.mine[s].wait()
        total = self.inbox[self.r, part].astype(F32)
        for i in (6, 4, 5, 1, 2, 3, 0):
            self.copy(i, self.came[i], s).wait_recv()
            total = total + self.inbox[self.came[i], part].astype(F32)
        return total

    def end(self):
        for copy in self.waiting:
            copy.wait_send()


def first_kernel(parts, w_first, b_first, w_second, strip, hidden, scaled,
                 inbox, outgoing, send, recv, local, gsend, grecv, glocal):
    r, c, z, yl, k = place()
    to, _ = row_peers(r)
    greet([(p, c) for p in to] + [(r, n) for n in col_neighbours(z, yl, k)])
    row_sum = RowSum(parts, inbox, PIECES, send, recv, local)
    gather = Gather(outgoing, strip, PIECES, gsend, grecv, glocal)

    def dense(slots):
        kept = []
        for slot in slots:
            high, low = halves(strip[slot])
            pre = dot(high, w_first[...]) + dot(low, w_first[...]) + b_first[...]
            kept.append(jnp.maximum(pre, 0.0).astype(BF16))
        products = [dot(one, w_second[...]).astype(BF16) for one in kept]
        for slot, one, product in zip(slots, kept, products):
            hidden[slot] = one
            scaled[slot] = product

    def of_stage(n):
        return [gather.slot(dz, other) for dz, other, _ in (gather.STAGES[n - 1] if n else ((0, False, ""),))]

    def of_twin(n):
        slots = [slot + 1 - 2 * k for slot in of_stage(n)]
        for slot in slots:
            for s in range(PIECES):
                gather.arrived(slot, s)
        return slots

    for s in range(PIECES):
        outgoing[gather.rows * s:gather.rows * (s + 1)] = row_sum.piece(s)
        gather.begin(s)
    for copy in gather.kept:
        copy.wait()
    dense(of_stage(0))
    for n in range(1, 6):
        for s in range(PIECES):
            gather.stage(n, s)
        dense(of_stage(n) + (of_twin(n - 1) if n < 5 else []))
        if n == 4:
            dense(of_twin(4))
    dense(of_twin(5))
    for copy in gather.started:
        copy.wait_send()
    row_sum.end()


def first_call(parts, w_first, b_first, w_second):
    return pl.pallas_call(
        first_kernel,
        out_shape=(
            jax.ShapeDtypeStruct((32, 256, 128), F32),
            jax.ShapeDtypeStruct((32, 256, 256), BF16),
            jax.ShapeDtypeStruct((32, 256, 128), BF16),
        ),
        in_specs=[ANY, VM, VM, VM],
        out_specs=(VM, VM, VM),
        scratch_shapes=[
            pltpu.VMEM((8, 256, 128), F32),
            pltpu.VMEM((256, 128), F32),
            pltpu.SemaphoreType.DMA((7, PIECES)),
            pltpu.SemaphoreType.DMA((7, PIECES)),
            pltpu.SemaphoreType.DMA((PIECES,)),
        ] + gather_scratch(PIECES),
        compiler_params=pltpu.CompilerParams(collective_id=1, has_side_effects=True, vmem_limit_bytes=LIMIT),
        name="first_layer",
    )(parts, w_first, b_first, w_second)


def second_kernel(parts, labels, train, b_second, logits, stats, grads,
                  inbox, outgoing, send, recv, local, gsend, grecv, glocal):
    r, c, z, yl, k = place()
    to, came = row_peers(r)
    greet([(p, c) for p in to])
    row_sum = RowSum(parts, inbox, 2, send, recv, local)
    classes = lax.broadcasted_iota(jnp.int32, (128, 256), 0)
    onehot = jnp.where(classes == labels[...], 1.0, 0.0).T
    mask = jnp.broadcast_to(train[...].astype(F32), (128, 256)).T
    count = 32768.0
    sends, mine = [], []
    stats[...] = jnp.zeros(stats.shape, F32)

    def grad_copy(i, slot, s):
        return remote(outgoing.at[s], grads.at[slot, s], gsend.at[i, s], grecv.at[i, s], to[i], c)

    for s in range(2):
        part = slice(128 * s, 128 * s + 128)
        scores = row_sum.piece(s) + b_second[...]
        row_max = jnp.max(scores, axis=1, keepdims=True)
        log_total = jnp.log(jnp.sum(jnp.exp(scores - row_max), axis=1, keepdims=True)) + row_max
        d_scores = mask[part] * (jnp.exp(scores - log_total) - onehot[part]) / count
        outgoing[s] = d_scores.astype(BF16)
        for i in range(7):
            sends.append(grad_copy(i, r, s))
            sends[-1].start()
        mine.append(pltpu.make_async_copy(outgoing.at[s], grads.at[r, s], glocal.at[s]))
        mine[-1].start()
        logits[part] = scores.astype(BF16)
        cross = mask[part] * onehot[part] * (log_total - scores) / count
        stats[0:1] += jnp.sum(d_scores, axis=0, keepdims=True)
        stats[1:2] += jnp.sum(cross, axis=0, keepdims=True)
    for s in range(2):
        for i in range(7):
            grad_copy(i, came[i], s).wait_recv()
        mine[s].wait()
    row_sum.end()
    for copy in sends:
        copy.wait_send()


def second_call(parts, labels, train, b_second):
    return pl.pallas_call(
        second_kernel,
        out_shape=(
            jax.ShapeDtypeStruct((256, 128), BF16),
            jax.ShapeDtypeStruct((8, 128), F32),
            jax.ShapeDtypeStruct((8, 2, 128, 128), BF16),
        ),
        in_specs=[ANY, VM, VM, VM],
        out_specs=(VM, VM, VM),
        scratch_shapes=[
            pltpu.VMEM((8, 256, 128), BF16),
            pltpu.VMEM((2, 128, 128), BF16),
        ] + 2 * [
            pltpu.SemaphoreType.DMA((7, 2)),
            pltpu.SemaphoreType.DMA((7, 2)),
            pltpu.SemaphoreType.DMA((2,)),
        ],
        compiler_params=pltpu.CompilerParams(collective_id=2, has_side_effects=True, vmem_limit_bytes=LIMIT),
        name="second_layer",
    )(parts, labels, train, b_second)


PIECE = 17


def weight_gradients(total, agg, hidden, w_second, stats, pay, g_first, g_second, g_bias):
    nodes = STEP // 128
    w_second_t = w_second[...].astype(F32).T.astype(BF16)
    g_first[...] = jnp.zeros(g_first.shape, F32)
    g_second[...] = jnp.zeros(g_second.shape, F32)
    g_bias[...] = jnp.zeros(g_bias.shape, F32)

    @pl.loop(0, hidden.shape[0] // nodes)
    def _(i):
        part = pl.ds(i * nodes, nodes)
        grad = total[part].reshape(STEP, 128).astype(BF16)
        kept = hidden[part].reshape(STEP, 256)
        d_pre = jnp.where(kept > 0, dot(grad, w_second_t), 0.0)
        g_second[...] += dot_tn(kept, grad)
        g_first[...] += dot_tn(agg[part].reshape(STEP, 128).astype(BF16), d_pre.astype(BF16))
        g_bias[...] += jnp.sum(d_pre.reshape(STEP // 8, 8, 256), axis=0)

    for p in range(8):
        pay[p, 0:16] = g_first[16 * p:16 * p + 16, 0:128]
        pay[p + 8, 0:16] = g_first[16 * p:16 * p + 16, 128:256]
    for p in range(16):
        pay[p + 16, 0:16] = g_second[16 * p:16 * p + 16]
    for p in range(4, 32):
        pay[p, 16:17] = jnp.zeros((1, 128), F32)
    bias = jnp.sum(g_bias[...], axis=0, keepdims=True)
    pay[0, 16:17] = stats[0:1]
    pay[1, 16:17] = stats[1:2]
    pay[2, 16:17] = bias[:, 0:128]
    pay[3, 16:17] = bias[:, 128:256]


def last_kernel(total_back, agg, hidden, w_second, stats, sums, pay, g_first, g_second, g_bias, box_t, half, box_p, box_z, t_send, t_recv, p_send, p_recv, z_send, z_recv):
    r, c, z, yl, k = place()
    me, mine16 = 4 * (r % 4) + 2 * (r // 4) + yl, 16 * k

    def on_plane(j):
        return 4 * (j % 4 // 2) + j // 4, 4 * z + 2 * (j % 2) + k

    def on_z(j):
        return r, 4 * j + 2 * yl + k

    def others(n, first, then):
        @pl.loop(1, n)
        def _(i):
            then(lax.rem(first + i, n))

    barrier = pltpu.get_barrier_semaphore()

    def signal(device):
        pl.semaphore_signal(barrier, inc=1, device_id=device, device_id_type=MESH)

    others(8, z, lambda j: signal(on_z(j)))
    others(16, me, lambda j: signal(on_plane(j)))
    twin = (r, 4 * z + 2 * yl + 1 - k)
    signal(twin)
    weight_gradients(total_back, agg, hidden, w_second, stats, pay, g_first, g_second, g_bias)
    pl.semaphore_wait(barrier, 23)

    half_copy = remote(pay.at[pl.ds(16 - mine16, 16)], box_t, t_send.at[0], t_recv.at[0], *twin)
    half_copy.start()
    half_copy.wait_recv()
    half[...] = pay[pl.ds(mine16, 16)] + box_t[...]

    def plane_copy(j, frm):
        return remote(half.at[j], box_p.at[frm], p_send.at[0, j], p_recv.at[0, frm], *on_plane(j))

    def z_copy(j, frm):
        return remote(box_z.at[z], box_z.at[frm], z_send.at[j], z_recv.at[frm], *on_z(j))

    def plane_back(j, frm):
        block = sums.at[mine16 + frm]
        return remote(block, block, p_send.at[1, j], p_recv.at[1, frm], *on_plane(j))

    others(16, me, lambda j: plane_copy(j, me).start())
    box_p[me] = half[me]
    others(16, me, lambda j: plane_copy(j, j).wait_recv())
    total = box_p[0]
    for j in range(1, 16):
        total = total + box_p[j]
    box_z[z] = total
    others(8, z, lambda j: z_copy(j, z).start())
    others(8, z, lambda j: z_copy(j, j).wait_recv())
    total = box_z[0]
    for j in range(1, 8):
        total = total + box_z[j]
    sums[mine16 + me] = total
    others(16, me, lambda j: plane_back(j, me).start())
    others(16, me, lambda j: plane_back(j, j).wait_recv())
    back = sums.at[pl.ds(mine16, 16)]
    back_copy = remote(back, back, t_send.at[1], t_recv.at[1], *twin)
    back_copy.start()
    other_half = sums.at[pl.ds(16 - mine16, 16)]
    remote(other_half, other_half, t_send.at[1], t_recv.at[1], *twin).wait_recv()
    half_copy.wait_send()
    back_copy.wait_send()
    others(8, z, lambda j: z_copy(j, z).wait_send())
    others(16, me, lambda j: plane_copy(j, me).wait_send())
    others(16, me, lambda j: plane_back(j, me).wait_send())


def last_call(*dense):
    return pl.pallas_call(
        last_kernel,
        out_shape=jax.ShapeDtypeStruct((32, PIECE, 128), F32),
        in_specs=[VM] * 5,
        out_specs=VM,
        scratch_shapes=[
            pltpu.VMEM((32, PIECE, 128), F32),
            pltpu.VMEM((128, 256), F32),
            pltpu.VMEM((256, 128), F32),
            pltpu.VMEM((8, 256), F32),
            pltpu.VMEM((16, PIECE, 128), F32),
            pltpu.VMEM((16, PIECE, 128), F32),
            pltpu.VMEM((16, PIECE, 128), F32),
            pltpu.VMEM((8, PIECE, 128), F32),
            pltpu.SemaphoreType.DMA((2,)),
            pltpu.SemaphoreType.DMA((2,)),
            pltpu.SemaphoreType.DMA((2, 16)),
            pltpu.SemaphoreType.DMA((2, 16)),
            pltpu.SemaphoreType.DMA((8,)),
            pltpu.SemaphoreType.DMA((8,)),
        ],
        compiler_params=pltpu.CompilerParams(collective_id=3, has_side_effects=True, vmem_limit_bytes=LIMIT),
        name="weight_gradients",
    )(*dense)


def finish_kernel(sums, scores, logits, loss, g_first, b_first, g_second, b_second):
    logits[...] = scores[...]
    for p in range(8):
        g_first[16 * p:16 * p + 16, 0:128] = sums[p, 0:16]
        g_first[16 * p:16 * p + 16, 128:256] = sums[p + 8, 0:16]
    for p in range(16):
        g_second[16 * p:16 * p + 16] = sums[p + 16, 0:16]
    b_second[...] = sums[0, 16:17]
    loss[...] = jnp.sum(sums[1, 16:17], axis=1, keepdims=True)
    b_first[:, 0:128] = sums[2, 16:17]
    b_first[:, 128:256] = sums[3, 16:17]


def finish_call(sums, scores):
    return pl.pallas_call(
        finish_kernel,
        out_shape=(
            jax.ShapeDtypeStruct((256, 128), BF16),
            jax.ShapeDtypeStruct((1, 1), F32),
            jax.ShapeDtypeStruct((128, 256), F32),
            jax.ShapeDtypeStruct((1, 256), F32),
            jax.ShapeDtypeStruct((256, 128), F32),
            jax.ShapeDtypeStruct((1, 128), F32),
        ),
        in_specs=[VM, VM],
        out_specs=(VM,) * 6,
        compiler_params=pltpu.CompilerParams(vmem_limit_bytes=4 * 1024 * 1024),
        name="outputs",
    )(sums, scores)


def local(features, labels, train_mask, adj_rows, adj_cols, adj_live, adj_values, w_first, b_first, w_second, b_second):
    strip, blocks = gather_call(features, adj_values[0, 0])
    index = (adj_rows, adj_cols, adj_live, blocks)
    shape = jax.ShapeDtypeStruct
    part = product_call(
        product_first_kernel, index, (strip.reshape(64, 128, 128),), shape((16, 128, 128), F32), [pltpu.VMEM((17, 128, 128), F32)],
        "product_first",
    )
    agg, hidden, scaled = first_call(part.reshape(8, 256, 128), w_first, b_first.reshape(1, 256), w_second)
    part = product_call(
        product_second_kernel, index, (scaled.reshape(64, 128, 128),), shape((16, 128, 128), BF16),
        [pltpu.VMEM((17, 128, 128), F32)], "product_second",
    )
    scores, stats, grads = second_call(
        part.reshape(8, 256, 128), labels.reshape(1, 256), train_mask.reshape(1, 256), b_second.reshape(1, 128)
    )
    total = product_call(
        product_back_kernel, index, (grads.reshape(16, 128, 128),), shape((65, 128, 128), F32), [], "product_back"
    )
    sums = last_call(total, agg.reshape(64, 128, 128), hidden.reshape(64, 128, 256), w_second, stats)
    logits, loss, g_first, gb_first, g_second, gb_second = finish_call(sums, scores)
    return logits, loss.reshape(()), g_first, gb_first.reshape(256), g_second, gb_second.reshape(128)


def solution(mesh):
    in_specs = (
        P(("row", "col"), None),
        P(("row", "col")),
        P(("row", "col")),
        P("row", "col", None),
        P("row", "col", None),
        P("row", "col"),
        P("row", "col", None, None, None),
        P(),
        P(),
        P(),
        P(),
    )
    out_specs = (P(("row", "col"), None), P(), P(), P(), P(), P())
    return jax.shard_map(local, mesh=mesh, in_specs=in_specs, out_specs=out_specs, check_vma=False)
```

```python
import functools

import jax
import jax.numpy as jnp
from jax import lax
from jax.experimental import pallas as pl
from jax.experimental.pallas import tpu as pltpu
from jax.sharding import PartitionSpec as P

MESH = pl.DeviceIdType.MESH
F32, BF16 = jnp.float32, jnp.bfloat16
ANY = pl.BlockSpec(memory_space=pl.ANY)
VM = pl.BlockSpec(memory_space=pltpu.VMEM)
SM = pl.BlockSpec(memory_space=pltpu.SMEM)
LIMIT = 32 * 1024 * 1024
PRODUCT_LIMIT = 24 * 1024 * 1024
UNROLL = 32
STEP = 4096
PIECES, STAGGER = 2, False
LOADS = 4


def dot(a, b):
    return jnp.dot(a, b, preferred_element_type=F32)


def dot_tn(a, b):
    return lax.dot_general(a, b, (((0,), (0,)), ((), ())), preferred_element_type=F32)


def halves(a):
    hi = a.astype(BF16)
    return hi, (a - hi.astype(F32)).astype(BF16)


def place():
    r, c = lax.axis_index("row"), lax.axis_index("col")
    return r, c, c // 4, (c // 2) % 2, c % 2


def remote(src, dst, send, recv, r, c):
    return pltpu.make_async_remote_copy(
        src_ref=src, dst_ref=dst, send_sem=send, recv_sem=recv,
        device_id=(r, c), device_id_type=MESH,
    )


def col_neighbours(z, yl, k):
    up, down = (z + 1) % 8, (z + 7) % 8
    return (4 * up + 2 * yl + k, 4 * down + 2 * yl + k, 4 * z + 2 * (1 - yl) + k, 4 * z + 2 * yl + 1 - k)


def second_neighbours(z, yl, k):
    return 4 * ((z + 2) % 8) + 2 * yl + k, 4 * ((z + 6) % 8) + 2 * yl + k


def row_peers(r):
    x, yh = r % 4, r // 4
    to, came = [], []
    for dy, dx in ((1, 2), (0, 2), (1, 1), (1, 3), (0, 1), (0, 3), (1, 0)):
        y2 = (yh + dy) % 2
        to.append(4 * y2 + (x + dx) % 4)
        came.append(4 * y2 + (x + 4 - dx) % 4)
    return to, came


def greet(devices):
    barrier = pltpu.get_barrier_semaphore()
    for device in devices:
        pl.semaphore_signal(barrier, inc=1, device_id=device, device_id_type=MESH)
    pl.semaphore_wait(barrier, len(devices))


def gather_scratch(pieces):
    return [
        pltpu.SemaphoreType.DMA((36 * pieces,)),
        pltpu.SemaphoreType.DMA((32, pieces)),
        pltpu.SemaphoreType.DMA((pieces,)),
    ]


class Gather:
    STAGES = (
        ((-1, False, "ut"), (1, False, "dt"), (0, True, "udt")),
        ((-2, False, "uat"), (2, False, "dt"), (1, True, "dt"), (-1, True, "t")),
        ((-3, False, "uat"), (3, False, "at"), (2, True, "t"), (-2, True, "t")),
        ((-4, False, "at"), (-3, True, "t"), (3, True, "t")),
        ((-4, True, "t"),),
    )

    DIRECT = (
        ((-1, False, "at"), (1, False, "at"), (0, True, "t")),
        ((-2, False, "uUat"), (2, False, "dat")),
        ((-1, True, "t"), (1, True, "t"), (-2, True, "t"), (2, True, "t")),
        ((-3, False, "at"), (3, False, "at")),
        ((-4, False, "at"),),
        ((-3, True, "t"), (3, True, "t"), (-4, True, "t")),
    )

    def __init__(self, src, out, pieces, send, recv, local):
        self.src, self.out, self.pieces, self.send, self.recv, self.local = src, out, pieces, send, recv, local
        self.rows = src.shape[0] // pieces
        self.r, self.c, self.z, self.yl, self.k = place()
        up, down, across, twin = col_neighbours(self.z, self.yl, self.k)
        up2, down2 = second_neighbours(self.z, self.yl, self.k)
        self.to = {"u": up, "d": down, "a": across, "t": twin, "U": up2, "D": down2}
        self.started, self.kept = [], []

    def slot(self, dz, other):
        return 4 * ((self.z + dz + 8) % 8) + 2 * (1 - self.yl if other else self.yl) + self.k

    def part(self, slot, s):
        return self.out.at[slot, pl.ds(s * self.rows, self.rows)]

    def push(self, block, slot, s, targets):
        for name in targets:
            copy = remote(block, self.part(slot, s), self.send.at[len(self.started)], self.recv.at[slot, s], self.r, self.to[name])
            copy.start()
            self.started.append(copy)

    def arrived(self, slot, s):
        block = self.part(slot, s)
        remote(block, block, self.send.at[0], self.recv.at[slot, s], self.r, self.to["t"]).wait_recv()

    def begin(self, s, targets="udat"):
        block = self.src.at[pl.ds(s * self.rows, self.rows)]
        self.push(block, self.c, s, targets)
        mine = pltpu.make_async_copy(block, self.part(self.c, s), self.local.at[s])
        mine.start()
        self.kept.append(mine)

    def stage(self, n, s, stages=STAGES):
        for dz, other, targets in stages[n - 1]:
            slot = self.slot(dz, other)
            self.arrived(slot, s)
            self.push(self.part(slot, s), slot, s, targets)

    def end(self):
        for s in range(self.pieces):
            for dz in range(8):
                for other in (False, True):
                    self.arrived(self.slot(dz, other) + 1 - 2 * self.k, s)
        for copy in self.kept:
            copy.wait()
        for copy in self.started:
            copy.wait_send()


def gather_kernel(src, blocks, out, held, load_sem, *sems):
    r, c, z, yl, k = place()
    greet([(r, n) for n in col_neighbours(z, yl, k) + second_neighbours(z, yl, k)])
    gather = Gather(src, out, 1, *sems)
    gather.begin(0, "audUDt")
    share = blocks.shape[0] // LOADS
    loads = [
        pltpu.make_async_copy(blocks.at[pl.ds(i * share, share)], held.at[pl.ds(i * share, share)], load_sem.at[i])
        for i in range(LOADS)
    ]
    for load in loads:
        load.start()
    for n in range(1, 7):
        gather.stage(n, 0, gather.DIRECT)
    gather.end()
    for load in loads:
        load.wait()


def gather_call(features, blocks):
    return pl.pallas_call(
        gather_kernel,
        out_shape=(
            jax.ShapeDtypeStruct((32,) + features.shape, BF16),
            jax.ShapeDtypeStruct(blocks.shape, BF16),
        ),
        in_specs=[ANY, ANY],
        out_specs=(VM, VM),
        scratch_shapes=[pltpu.SemaphoreType.DMA((LOADS,))] + gather_scratch(1),
        compiler_params=pltpu.CompilerParams(collective_id=0, has_side_effects=True, vmem_limit_bytes=LIMIT),
        name="gather_features",
    )(pltpu.with_memory_space_constraint(features, pltpu.HBM), pltpu.with_memory_space_constraint(blocks, pltpu.HBM))


def sparse_product(backward, rows, cols, live, blocks, source, total):
    n = jnp.max(live[...])
    outs = total.shape[0] - 1

    @pl.loop(0, outs, unroll=2)
    def _(i):
        total[i] = jnp.zeros(total.shape[1:], F32)

    @pl.loop(0, (n + UNROLL - 1) // UNROLL)
    def _(u):
        products, targets = [], []
        for i in range(UNROLL):
            b = u * UNROLL + i
            row, col = rows[0, 0, b], cols[0, 0, b]
            if backward:
                products.append(dot_tn(blocks[b], source[row]))
                targets.append(jnp.where(b < n, col, outs))
            else:
                products.append(dot(blocks[b], source[col]))
                targets.append(jnp.where(b < n, row, outs))
        for product, target in zip(products, targets):
            total[target] += product


def product_first_kernel(rows, cols, live, blocks, source, out, total):
    sparse_product(False, rows, cols, live, blocks, source, total)

    @pl.loop(0, out.shape[0], unroll=2)
    def _(i):
        out[i] = total[i]


def product_second_kernel(rows, cols, live, blocks, source, out, total):
    sparse_product(False, rows, cols, live, blocks, source, total)

    @pl.loop(0, out.shape[0], unroll=2)
    def _(i):
        out[i] = total[i].astype(BF16)


def product_back_kernel(rows, cols, live, blocks, source, total):
    sparse_product(True, rows, cols, live, blocks, source, total)


def product_call(kernel, index, dense, out_shape, scratch, name):
    return pl.pallas_call(
        kernel,
        out_shape=out_shape,
        in_specs=[SM, SM] + [VM] * (2 + len(dense)),
        out_specs=jax.tree.map(lambda _: VM, out_shape),
        scratch_shapes=scratch,
        compiler_params=pltpu.CompilerParams(vmem_limit_bytes=PRODUCT_LIMIT),
        name=name,
    )(*index, *dense)


class RowSum:
    def __init__(self, parts, inbox, pieces, send, recv, local):
        self.parts, self.inbox, self.send, self.recv, self.local = parts, inbox, send, recv, local
        self.rows = inbox.shape[1] // pieces
        self.r, self.c, _, _, _ = place()
        self.to, self.came = row_peers(self.r)
        self.copies, self.mine = [], []
        for s in range(pieces):
            if s and STAGGER:
                for copy in self.copies:
                    copy.wait_send()
            for i in range(7):
                self.copies.append(self.copy(i, self.r, s))
                self.copies[-1].start()
            part = pl.ds(s * self.rows, self.rows)
            self.mine.append(pltpu.make_async_copy(parts.at[self.r, part], inbox.at[self.r, part], local.at[s]))
            self.mine[-1].start()
        self.waiting = self.copies[7 * (pieces - 1):] if STAGGER else self.copies

    def copy(self, i, slot, s):
        part = pl.ds(s * self.rows, self.rows)
        return remote(self.parts.at[self.to[i], part], self.inbox.at[slot, part], self.send.at[i, s], self.recv.at[i, s], self.to[i], self.c)

    def piece(self, s):
        part = slice(s * self.rows, (s + 1) * self.rows)
        self.mine[s].wait()
        total = self.inbox[self.r, part].astype(F32)
        for i in (6, 4, 5, 1, 2, 3, 0):
            self.copy(i, self.came[i], s).wait_recv()
            total = total + self.inbox[self.came[i], part].astype(F32)
        return total

    def end(self):
        for copy in self.waiting:
            copy.wait_send()


def first_kernel(parts, w_first, b_first, w_second, rounded, hidden, scaled,
                 strip, inbox, outgoing, send, recv, local, gsend, grecv, glocal):
    r, c, z, yl, k = place()
    to, _ = row_peers(r)
    greet([(p, c) for p in to] + [(r, n) for n in col_neighbours(z, yl, k)])
    row_sum = RowSum(parts, inbox, PIECES, send, recv, local)
    gather = Gather(outgoing, strip, PIECES, gsend, grecv, glocal)

    def dense(slots):
        kept = []
        for slot in slots:
            high, low = halves(strip[slot])
            rounded[slot] = high
            pre = dot(high, w_first[...]) + dot(low, w_first[...]) + b_first[...]
            kept.append(jnp.maximum(pre, 0.0).astype(BF16))
        products = [dot(one, w_second[...]).astype(BF16) for one in kept]
        for slot, one, product in zip(slots, kept, products):
            hidden[slot] = one
            scaled[slot] = product

    def of_stage(n):
        return [gather.slot(dz, other) for dz, other, _ in (gather.STAGES[n - 1] if n else ((0, False, ""),))]

    def of_twin(n):
        slots = [slot + 1 - 2 * k for slot in of_stage(n)]
        for slot in slots:
            for s in range(PIECES):
                gather.arrived(slot, s)
        return slots

    for s in range(PIECES):
        outgoing[gather.rows * s:gather.rows * (s + 1)] = row_sum.piece(s)
        gather.begin(s)
    for copy in gather.kept:
        copy.wait()
    dense(of_stage(0))
    for n in range(1, 6):
        for s in range(PIECES):
            gather.stage(n, s)
        dense(of_stage(n) + (of_twin(n - 1) if n < 5 else []))
        if n == 4:
            dense(of_twin(4))
    dense(of_twin(5))
    for copy in gather.started:
        copy.wait_send()
    row_sum.end()


def first_call(parts, w_first, b_first, w_second):
    return pl.pallas_call(
        first_kernel,
        out_shape=(
            jax.ShapeDtypeStruct((32, 256, 128), BF16),
            jax.ShapeDtypeStruct((32, 256, 256), BF16),
            jax.ShapeDtypeStruct((32, 256, 128), BF16),
        ),
        in_specs=[ANY, VM, VM, VM],
        out_specs=(VM, VM, VM),
        scratch_shapes=[
            pltpu.VMEM((32, 256, 128), F32),
            pltpu.VMEM((8, 256, 128), F32),
            pltpu.VMEM((256, 128), F32),
            pltpu.SemaphoreType.DMA((7, PIECES)),
            pltpu.SemaphoreType.DMA((7, PIECES)),
            pltpu.SemaphoreType.DMA((PIECES,)),
        ] + gather_scratch(PIECES),
        compiler_params=pltpu.CompilerParams(collective_id=1, has_side_effects=True, vmem_limit_bytes=LIMIT),
        name="first_layer",
    )(parts, w_first, b_first, w_second)


def second_kernel(parts, labels, train, b_second, logits, stats, grads,
                  inbox, outgoing, send, recv, local, gsend, grecv, glocal):
    r, c, z, yl, k = place()
    to, came = row_peers(r)
    greet([(p, c) for p in to])
    row_sum = RowSum(parts, inbox, 2, send, recv, local)
    classes = lax.broadcasted_iota(jnp.int32, (128, 256), 0)
    onehot = jnp.where(classes == labels[...], 1.0, 0.0).T
    mask = jnp.broadcast_to(train[...].astype(F32), (128, 256)).T
    count = 32768.0
    sends, mine = [], []
    stats[...] = jnp.zeros(stats.shape, F32)

    def grad_copy(i, slot, s):
        return remote(outgoing.at[s], grads.at[slot, s], gsend.at[i, s], grecv.at[i, s], to[i], c)

    for s in range(2):
        part = slice(128 * s, 128 * s + 128)
        scores = row_sum.piece(s) + b_second[...]
        row_max = jnp.max(scores, axis=1, keepdims=True)
        log_total = jnp.log(jnp.sum(jnp.exp(scores - row_max), axis=1, keepdims=True)) + row_max
        d_scores = mask[part] * (jnp.exp(scores - log_total) - onehot[part]) / count
        outgoing[s] = d_scores.astype(BF16)
        for i in range(7):
            sends.append(grad_copy(i, r, s))
            sends[-1].start()
        mine.append(pltpu.make_async_copy(outgoing.at[s], grads.at[r, s], glocal.at[s]))
        mine[-1].start()
        logits[part] = scores.astype(BF16)
        cross = mask[part] * onehot[part] * (log_total - scores) / count
        stats[0:1] += jnp.sum(d_scores, axis=0, keepdims=True)
        stats[1:2] += jnp.sum(cross, axis=0, keepdims=True)
    for s in range(2):
        for i in range(7):
            grad_copy(i, came[i], s).wait_recv()
        mine[s].wait()
    row_sum.end()
    for copy in sends:
        copy.wait_send()


def second_call(parts, labels, train, b_second):
    return pl.pallas_call(
        second_kernel,
        out_shape=(
            jax.ShapeDtypeStruct((256, 128), BF16),
            jax.ShapeDtypeStruct((8, 128), F32),
            jax.ShapeDtypeStruct((8, 2, 128, 128), BF16),
        ),
        in_specs=[ANY, VM, VM, VM],
        out_specs=(VM, VM, VM),
        scratch_shapes=[
            pltpu.VMEM((8, 256, 128), BF16),
            pltpu.VMEM((2, 128, 128), BF16),
        ] + 2 * [
            pltpu.SemaphoreType.DMA((7, 2)),
            pltpu.SemaphoreType.DMA((7, 2)),
            pltpu.SemaphoreType.DMA((2,)),
        ],
        compiler_params=pltpu.CompilerParams(collective_id=2, has_side_effects=True, vmem_limit_bytes=LIMIT),
        name="second_layer",
    )(parts, labels, train, b_second)


PIECE = 17


def weight_gradients(total, agg, hidden, w_second, stats, pay, g_first, g_second, g_bias):
    nodes = STEP // 128
    w_second_t = w_second[...].astype(F32).T.astype(BF16)
    g_first[...] = jnp.zeros(g_first.shape, F32)
    g_second[...] = jnp.zeros(g_second.shape, F32)
    g_bias[...] = jnp.zeros(g_bias.shape, F32)

    @pl.loop(0, hidden.shape[0] // nodes)
    def _(i):
        part = pl.ds(i * nodes, nodes)
        grad = total[part].reshape(STEP, 128).astype(BF16)
        kept = hidden[part].reshape(STEP, 256)
        d_pre = jnp.where(kept > 0, dot(grad, w_second_t), 0.0)
        g_second[...] += dot_tn(kept, grad)
        g_first[...] += dot_tn(agg[part].reshape(STEP, 128), d_pre.astype(BF16))
        g_bias[...] += jnp.sum(d_pre.reshape(STEP // 8, 8, 256), axis=0)

    for p in range(8):
        pay[p, 0:16] = g_first[16 * p:16 * p + 16, 0:128]
        pay[p + 8, 0:16] = g_first[16 * p:16 * p + 16, 128:256]
    for p in range(16):
        pay[p + 16, 0:16] = g_second[16 * p:16 * p + 16]
    for p in range(4, 32):
        pay[p, 16:17] = jnp.zeros((1, 128), F32)
    bias = jnp.sum(g_bias[...], axis=0, keepdims=True)
    pay[0, 16:17] = stats[0:1]
    pay[1, 16:17] = stats[1:2]
    pay[2, 16:17] = bias[:, 0:128]
    pay[3, 16:17] = bias[:, 128:256]


def last_kernel(total_back, agg, hidden, w_second, stats, sums, pay, g_first, g_second, g_bias, box_t, half, box_p, box_z, t_send, t_recv, p_send, p_recv, z_send, z_recv):
    r, c, z, yl, k = place()
    me, mine16 = 4 * (r % 4) + 2 * (r // 4) + yl, 16 * k

    def on_plane(j):
        return 4 * (j % 4 // 2) + j // 4, 4 * z + 2 * (j % 2) + k

    def on_z(j):
        return r, 4 * j + 2 * yl + k

    def others(n, first, then):
        @pl.loop(1, n)
        def _(i):
            then(lax.rem(first + i, n))

    barrier = pltpu.get_barrier_semaphore()

    def signal(device):
        pl.semaphore_signal(barrier, inc=1, device_id=device, device_id_type=MESH)

    others(8, z, lambda j: signal(on_z(j)))
    others(16, me, lambda j: signal(on_plane(j)))
    twin = (r, 4 * z + 2 * yl + 1 - k)
    signal(twin)
    weight_gradients(total_back, agg, hidden, w_second, stats, pay, g_first, g_second, g_bias)
    pl.semaphore_wait(barrier, 23)

    half_copy = remote(pay.at[pl.ds(16 - mine16, 16)], box_t, t_send.at[0], t_recv.at[0], *twin)
    half_copy.start()
    half_copy.wait_recv()
    half[...] = pay[pl.ds(mine16, 16)] + box_t[...]

    def plane_copy(j, frm):
        return remote(half.at[j], box_p.at[frm], p_send.at[0, j], p_recv.at[0, frm], *on_plane(j))

    def z_copy(j, frm):
        return remote(box_z.at[z], box_z.at[frm], z_send.at[j], z_recv.at[frm], *on_z(j))

    def plane_back(j, frm):
        block = sums.at[mine16 + frm]
        return remote(block, block, p_send.at[1, j], p_recv.at[1, frm], *on_plane(j))

    others(16, me, lambda j: plane_copy(j, me).start())
    box_p[me] = half[me]
    others(16, me, lambda j: plane_copy(j, j).wait_recv())
    total = box_p[0]
    for j in range(1, 16):
        total = total + box_p[j]
    box_z[z] = total
    others(8, z, lambda j: z_copy(j, z).start())
    others(8, z, lambda j: z_copy(j, j).wait_recv())
    total = box_z[0]
    for j in range(1, 8):
        total = total + box_z[j]
    sums[mine16 + me] = total
    others(16, me, lambda j: plane_back(j, me).start())
    others(16, me, lambda j: plane_back(j, j).wait_recv())
    back = sums.at[pl.ds(mine16, 16)]
    back_copy = remote(back, back, t_send.at[1], t_recv.at[1], *twin)
    back_copy.start()
    other_half = sums.at[pl.ds(16 - mine16, 16)]
    remote(other_half, other_half, t_send.at[1], t_recv.at[1], *twin).wait_recv()
    half_copy.wait_send()
    back_copy.wait_send()
    others(8, z, lambda j: z_copy(j, z).wait_send())
    others(16, me, lambda j: plane_copy(j, me).wait_send())
    others(16, me, lambda j: plane_back(j, me).wait_send())


def last_call(*dense):
    return pl.pallas_call(
        last_kernel,
        out_shape=jax.ShapeDtypeStruct((32, PIECE, 128), F32),
        in_specs=[VM] * 5,
        out_specs=VM,
        scratch_shapes=[
            pltpu.VMEM((32, PIECE, 128), F32),
            pltpu.VMEM((128, 256), F32),
            pltpu.VMEM((256, 128), F32),
            pltpu.VMEM((8, 256), F32),
            pltpu.VMEM((16, PIECE, 128), F32),
            pltpu.VMEM((16, PIECE, 128), F32),
            pltpu.VMEM((16, PIECE, 128), F32),
            pltpu.VMEM((8, PIECE, 128), F32),
            pltpu.SemaphoreType.DMA((2,)),
            pltpu.SemaphoreType.DMA((2,)),
            pltpu.SemaphoreType.DMA((2, 16)),
            pltpu.SemaphoreType.DMA((2, 16)),
            pltpu.SemaphoreType.DMA((8,)),
            pltpu.SemaphoreType.DMA((8,)),
        ],
        compiler_params=pltpu.CompilerParams(collective_id=3, has_side_effects=True, vmem_limit_bytes=LIMIT),
        name="weight_gradients",
    )(*dense)


def finish_kernel(sums, scores, logits, loss, g_first, b_first, g_second, b_second):
    logits[...] = scores[...]
    for p in range(8):
        g_first[16 * p:16 * p + 16, 0:128] = sums[p, 0:16]
        g_first[16 * p:16 * p + 16, 128:256] = sums[p + 8, 0:16]
    for p in range(16):
        g_second[16 * p:16 * p + 16] = sums[p + 16, 0:16]
    b_second[...] = sums[0, 16:17]
    loss[...] = jnp.sum(sums[1, 16:17], axis=1, keepdims=True)
    b_first[:, 0:128] = sums[2, 16:17]
    b_first[:, 128:256] = sums[3, 16:17]


def finish_call(sums, scores):
    return pl.pallas_call(
        finish_kernel,
        out_shape=(
            jax.ShapeDtypeStruct((256, 128), BF16),
            jax.ShapeDtypeStruct((1, 1), F32),
            jax.ShapeDtypeStruct((128, 256), F32),
            jax.ShapeDtypeStruct((1, 256), F32),
            jax.ShapeDtypeStruct((256, 128), F32),
            jax.ShapeDtypeStruct((1, 128), F32),
        ),
        in_specs=[VM, VM],
        out_specs=(VM,) * 6,
        compiler_params=pltpu.CompilerParams(vmem_limit_bytes=4 * 1024 * 1024),
        name="outputs",
    )(sums, scores)


def local(features, labels, train_mask, adj_rows, adj_cols, adj_live, adj_values, w_first, b_first, w_second, b_second):
    strip, blocks = gather_call(features, adj_values[0, 0])
    index = (adj_rows, adj_cols, adj_live, blocks)
    shape = jax.ShapeDtypeStruct
    part = product_call(
        product_first_kernel, index, (strip.reshape(64, 128, 128),), shape((16, 128, 128), F32), [pltpu.VMEM((17, 128, 128), F32)],
        "product_first",
    )
    agg, hidden, scaled = first_call(part.reshape(8, 256, 128), w_first, b_first.reshape(1, 256), w_second)
    part = product_call(
        product_second_kernel, index, (scaled.reshape(64, 128, 128),), shape((16, 128, 128), BF16),
        [pltpu.VMEM((17, 128, 128), F32)], "product_second",
    )
    scores, stats, grads = second_call(
        part.reshape(8, 256, 128), labels.reshape(1, 256), train_mask.reshape(1, 256), b_second.reshape(1, 128)
    )
    total = product_call(
        product_back_kernel, index, (grads.reshape(16, 128, 128),), shape((65, 128, 128), F32), [], "product_back"
    )
    sums = last_call(total, agg.reshape(64, 128, 128), hidden.reshape(64, 128, 256), w_second, stats)
    logits, loss, g_first, gb_first, g_second, gb_second = finish_call(sums, scores)
    return logits, loss.reshape(()), g_first, gb_first.reshape(256), g_second, gb_second.reshape(128)


def solution(mesh):
    in_specs = (
        P(("row", "col"), None),
        P(("row", "col")),
        P(("row", "col")),
        P("row", "col", None),
        P("row", "col", None),
        P("row", "col"),
        P("row", "col", None, None, None),
        P(),
        P(),
        P(),
        P(),
    )
    out_specs = (P(("row", "col"), None), P(), P(), P(), P(), P())
    return jax.shard_map(local, mesh=mesh, in_specs=in_specs, out_specs=out_specs, check_vma=False)
```
